256 devices in a mesh: row: 16 (over x, z_hi), col: 16 (over z_lo, y, core).
Axes of the slice: x: 4, y: 4, z: 8 (z_hi: 4, z_lo: 2; z = z_hi * 2 + z_lo), core: 2. Of those that a mesh axis runs over, the one named last changes fastest.
Arguments:
- observed: float32 [65536, 128], P('row'), may hold values from -6 to 6
- slip: float32 [32768, 256], P('col'), may hold values from 0 to 1.5
- green_left: bfloat16 [65536, 2048], P('row', 'col'), may hold values from -0.5 to 0.5
- green_right: bfloat16 [32768, 4096], P('col', 'row'), may hold values from -0.0234375 to 0.0234375
- block_ranks: int32 [16, 16], P('row', 'col'), may hold values from 32 to 128
- neighbours: int32 [32768, 8], P('col'), may hold values from 0 to 32767, as said below
Outputs:
- slip_next: float32 [32768, 256], P('col')
- residual: float32 [65536, 128], P('row')
The draws below stay inside these ranges and needn't reach their ends.
Inputs may be any that keep to these rules, and one draw needn't show every extreme that they name: `neighbours`: each entry lies within 64 patch numbers of its own patch; an entry equal to the patch itself is padding.
All inputs are finite; a program needn't handle non-finite values.
Results may differ from the reference program's by a relative error of at most 0.0037.
Values sent between devices are 32-bit elements; how exact they have to be, the bound alone decides.
A program may use at most 128 MiB of HBM per device.

```python
import jax
import jax.numpy as jnp
from jax import lax

NRHS = 128
KMAX = 128
HALO = 64
ROWS_DEV = 4096
PATCH_DEV = 2048
NDATA = 65536
NPATCH = 32768
N_ROW = 16
N_COL = 16


def draw_neighbours(key, part):
    key = jax.random.fold_in(key, 11)
    first, second, third = jax.random.split(key, 3)
    offsets = jax.random.randint(first, (NPATCH, 8), -HALO, HALO + 1)
    padding = jax.random.randint(second, (NPATCH, 8), 0, 4) == 0
    offsets = jnp.where(padding, 0, offsets)
    sign = jax.random.randint(third, (NPATCH,), 0, 2) * 2 - 1
    offsets = offsets.at[:, 0].set(sign * HALO)
    patch = jnp.arange(NPATCH, dtype=jnp.int32)[:, None]
    return jnp.clip(patch + offsets, 0, NPATCH - 1).astype(jnp.int32)


def set_ends(array, rng, low, largest):
    longest = array.shape.index(max(array.shape))
    spots = []
    for shift in (0, 1):
        where = [jax.random.randint(jax.random.fold_in(rng, axis), (), 0, length) for axis, length in enumerate(array.shape)]
        where[longest] = (where[longest] + shift) % array.shape[longest]
        spots.append(tuple(where))
    return array.at[spots[0]].set(low).at[spots[1]].set(largest)


def shard_levels(rng, extent, pieces, low, high):
    def one(axis_at, parts):
        heights = jax.random.uniform(jax.random.fold_in(jax.random.fold_in(rng, 6), axis_at), (parts,), jnp.float32, low / len(pieces), high / len(pieces))
        return jnp.repeat(jnp.exp(heights), extent[axis_at] // parts).reshape((-1,) + (1,) * (len(extent) - axis_at - 1))

    factor_of = one(*pieces[0])
    for cut in pieces[1:]:
        factor_of = factor_of * one(*cut)
    return factor_of


def centred(stream_key, shape, spread, reach, pieces=(), kind=jnp.bfloat16):
    loudness = shard_levels(stream_key, shape, pieces, -0.22, 0.18) if pieces else 1.0
    array = jax.random.normal(stream_key, shape, jnp.float32) * spread * loudness
    return jnp.minimum(jnp.maximum(array, -reach), reach).astype(kind)


def setup_inputs(seed: int = 0) -> dict:
    key_list = jax.random.split(jax.random.key(seed), 7)
    return {
        "observed": centred(key_list[0], (NDATA, NRHS), 1.0, 6.0, ((0, 16),), jnp.float32),
        "slip": jnp.clip(1.5 * jax.random.uniform(key_list[1], (NPATCH, 2 * NRHS), jnp.float32) ** shard_levels(key_list[1], (NPATCH, 2 * NRHS), ((0, 16),), -0.2, 0.2), 0.0, 1.5),
        "green_left": centred(key_list[2], (NDATA, N_COL * KMAX), KMAX ** -0.5, 0.5, ((0, 16), (1, 16))),
        "green_right": centred(key_list[3], (NPATCH, N_ROW * 2 * KMAX), (2 * NPATCH) ** -0.5, 0.0234375, ((0, 16), (1, 16))),
        "block_ranks": set_ends(jax.random.randint(key_list[4], (N_ROW, N_COL), KMAX // 4, KMAX + 1), jax.random.fold_in(key_list[4], 1), KMAX // 4, KMAX).astype(jnp.int32),
        "neighbours": draw_neighbours(jax.random.fold_in(key_list[6], 71), 0),
    }


def reference(observed, slip, green_left, green_right, block_ranks, neighbours):
    left = green_left.reshape(N_ROW, ROWS_DEV, N_COL, KMAX).astype(jnp.float32)
    right = green_right.reshape(N_COL, PATCH_DEV, N_ROW, 2, KMAX).astype(jnp.float32)
    slip_half = lax.optimization_barrier(slip.astype(jnp.bfloat16)).astype(jnp.float32)
    slip_half = slip_half.reshape(N_COL, PATCH_DEV, 2, NRHS)
    keep = (jnp.arange(KMAX, dtype=jnp.int32)[None, None, :] < block_ranks.T[:, :, None]).astype(jnp.float32)
    inner = jnp.einsum('cprak,cpan->crkn', right, slip_half) * keep[..., None]
    inner = lax.optimization_barrier(inner.astype(jnp.bfloat16)).astype(jnp.float32)
    predicted = jnp.einsum('rick,crkn->rin', left, inner).reshape(NDATA, NRHS)
    residual = predicted - observed
    res_half = lax.optimization_barrier(residual.astype(jnp.bfloat16)).astype(jnp.float32)
    res_half = res_half.reshape(N_ROW, ROWS_DEV, NRHS)
    back = jnp.einsum('rick,rin->rckn', left, res_half) * jnp.transpose(keep, (1, 0, 2))[..., None]
    back = lax.optimization_barrier(back.astype(jnp.bfloat16)).astype(jnp.float32)
    gradient = jnp.einsum('cprak,rckn->cpan', right, back).reshape(NPATCH, 2 * NRHS)
    smooth = 8.0 * slip
    for index in range(8):
        smooth = smooth - slip[neighbours[:, index]]
    slip_next = jnp.maximum(slip - 0.5 * (gradient + 0.05 * smooth), 0.0)
    return slip_next, residual
```

```python
import jax
import jax.numpy as jnp
from jax import lax
from jax.experimental import pallas as pl
from jax.experimental.pallas import tpu as pltpu
from jax.sharding import PartitionSpec as P

MESH = pl.DeviceIdType.MESH
F32 = jnp.float32
BF16 = jnp.bfloat16
HALO = 64
N_SEM = 160


def lane_low(shape):
    return lax.broadcasted_iota(jnp.int32, shape, 1) < 64


def swap_lanes(value):
    return pltpu.roll(value, 64, 1)


def ds(start, size, unit):
    if isinstance(start, int):
        return pl.ds(start, size)
    return pl.ds(pl.multiple_of(start, unit), size)


def kernel(
    obs, slip, gl, gr, rank, nbr, out, res,
    ext, glv, grv, obsv, nbrv, glsend, glrecv, xy, xyt, grsend, grrecv, grcat,
    insend, inrecv, rhs, pred, am1, ar, am3, zs, zr, resp, bsend, brecv, bx, bd, grad,
    cm1, cr, cm3, base, outp, outv, resv, send_sem, recv_sem, local_sem,
):
    row = lax.axis_index("row")
    col = lax.axis_index("col")
    x, zh = row // 4, row % 4
    zl, y, k = col // 8, (col // 2) % 4, col % 2

    def device(x, zh, zl, y, k):
        return (x * 4 + zh, (zl * 4 + y) * 2 + k)

    sibling = device(x, zh, zl, y, 1 - k)
    y_next = device(x, zh, zl, (y + 1) % 4, k)
    y_prev = device(x, zh, zl, (y + 3) % 4, k)
    z_pair = device(x, zh, 1 - zl, y, k)
    x_next = device((x + 1) % 4, zh, zl, y, k)
    x_prev = device((x + 3) % 4, zh, zl, y, k)
    x_far = device((x + 2) % 4, zh, zl, y, k)
    zh_next = device(x, (zh + 1) % 4, zl, y, k)
    zh_prev = device(x, (zh + 3) % 4, zl, y, k)
    col_next = (row, (col + 1) % 16)
    col_prev = (row, (col + 15) % 16)
    partners = (
        sibling, y_next, y_prev, z_pair, x_next, x_prev, x_far, zh_next, zh_prev, col_next, col_prev,
    )

    counts = [0, 0]
    sends = []

    def send(src, dst, to):
        index = counts[0]
        counts[0] += 1
        copy = pltpu.make_async_remote_copy(
            src_ref=src, dst_ref=dst, send_sem=send_sem.at[index], recv_sem=recv_sem.at[index],
            device_id=to, device_id_type=MESH,
        )
        copy.start()
        sends.append(copy)
        return copy

    def local(src, dst):
        index = counts[1]
        counts[1] += 1
        copy = pltpu.make_async_copy(src, dst, local_sem.at[index])
        copy.start()
        return copy

    load_gl = [
        local(gl.at[ds((1 - k) * 2048, 2048, 2048)], glv.at[pl.ds(2048, 2048)]),
    ]
    load_gr, load_slip = [], []
    for piece in range(4):
        rows = pl.ds(piece * 512, 512)
        load_gr.append(local(gr.at[rows], grv.at[rows]))
        load_slip.append(local(slip.at[rows], ext.at[pl.ds(HALO + piece * 512, 512)]))
    load_gl.append(local(gl.at[ds(k * 2048, 2048, 2048)], glv.at[pl.ds(0, 2048)]))
    shard = y * 256 + zl * 128
    load_obs = [
        local(obs.at[ds(k * 2048 + half * 1024 + shard, 128, 128)], obsv.at[half]) for half in range(2)
    ]
    load_nbr = local(nbr.at[:, ds(row * 128, 128, 128)], nbrv)

    barrier = pltpu.get_barrier_semaphore()
    for partner in partners:
        pl.semaphore_signal(barrier, inc=1, device_id=partner, device_id_type=MESH)

    load_gl[0].wait()

    def widen_left(i, carry):
        rows = ds(i * 256, 256, 256)
        glsend[rows, :] = glv[ds(2048 + i * 256, 256, 256), :].astype(F32)
        return carry

    lax.fori_loop(0, 8, widen_left, 0)
    pl.semaphore_wait(barrier, len(partners))
    swap_gl = [send(glsend.at[pl.ds(i * 512, 512)], glrecv.at[pl.ds(i * 512, 512)], sibling) for i in range(4)]

    keep = lax.broadcasted_iota(jnp.int32, (128, 128), 0) < rank[0, 0]

    inner = jnp.zeros((128, 128), F32)
    for piece in range(4):
        load_gr[piece].wait()
        load_slip[piece].wait()
        for rake in range(2):
            lanes = pl.ds(rake * 128, 128)
            inner += lax.dot_general(
                grv[pl.ds(piece * 512, 512), lanes],
                ext[pl.ds(HALO + piece * 512, 512), lanes].astype(BF16),
                (((0,), (0,)), ((), ())),
                preferred_element_type=F32,
            )
    inner = jnp.where(keep, inner, 0.0).astype(BF16).astype(F32)
    insend[...] = inner
    swap_inner = send(insend, inrecv, sibling)

    def widen_right(i, carry):
        rows = ds(i * 256, 256, 256)
        grsend[rows, :] = grv[rows, :].astype(F32)
        return carry

    lax.fori_loop(0, 8, widen_right, 0)

    def x_block(at):
        return ds(((x + at) % 4) * 512, 512, 512)

    share_gr = [
        send(grsend.at[x_block(3)], grrecv.at[0], x_prev),
        send(grsend.at[x_block(2)], grrecv.at[1], x_far),
        send(grsend.at[x_block(1)], grrecv.at[2], x_next),
    ]
    halo = [
        send(ext.at[pl.ds(2048, HALO)], ext.at[pl.ds(0, HALO)], col_next),
        send(ext.at[pl.ds(HALO, HALO)], ext.at[pl.ds(2048 + HALO, HALO)], col_prev),
    ]

    load_gl[1].wait()

    def own_left(i, carry):
        rows = ds(i * 256, 256, 256)
        xy[rows, pl.ds(0, 128)] = glv[rows, :]
        xy[rows, pl.ds(256, 128)] = glv[ds(1024 + i * 256, 256, 256), :]
        return carry

    lax.fori_loop(0, 4, own_left, 0)
    for copy in swap_gl:
        copy.wait_recv()

    def other_left(i, carry):
        rows = ds(i * 256, 256, 256)
        xy[rows, pl.ds(128, 128)] = glrecv[rows, :].astype(BF16)
        xy[rows, pl.ds(384, 128)] = glrecv[ds(1024 + i * 256, 256, 256), :].astype(BF16)
        return carry

    lax.fori_loop(0, 4, other_left, 0)
    for copy in load_obs:
        copy.wait()
    swap_inner.wait_recv()
    low = lane_low((256, 128))
    both = jnp.concatenate([inner, inrecv[...]], axis=0)
    turned = swap_lanes(both)
    rhs[0, pl.ds(0, 256), :] = jnp.where(low, both, 0.0).astype(BF16)
    rhs[0, pl.ds(256, 256), :] = jnp.where(low, 0.0, turned).astype(BF16)
    rhs[1, pl.ds(0, 256), :] = jnp.where(low, turned, 0.0).astype(BF16)
    rhs[1, pl.ds(256, 256), :] = jnp.where(low, 0.0, both).astype(BF16)

    def chain(h):
        values = pred.at[h]

        def predict(i, carry):
            rows = ds(i * 256, 256, 256)
            values[rows, :] = jnp.dot(xy[rows, :], rhs[h], preferred_element_type=F32)
            return carry

        lax.fori_loop(0, 4, predict, 0)

        def part(at, sub):
            return ds(((y + at) % 4) * 256 + sub * 128, 128, 128)

        up1 = send(values.at[part(2, 0)], am1.at[h, 0], y_next)
        down1 = send(values.at[part(2, 1)], am1.at[h, 1], y_prev)
        up2 = send(values.at[part(1, 1)], ar.at[h, 1, 0], y_next)
        down2 = send(values.at[part(3, 0)], ar.at[h, 0, 1], y_prev)
        yield 3.0
        up1.wait_recv()
        am3[h, 0] = values[part(1, 0), :] + am1[h, 0]
        up3 = send(am3.at[h, 0], ar.at[h, 0, 0], y_next)
        down1.wait_recv()
        am3[h, 1] = values[part(3, 1), :] + am1[h, 1]
        down3 = send(am3.at[h, 1], ar.at[h, 1, 1], y_prev)
        yield 5.7
        for copy in (up2, down2, up3, down3):
            copy.wait_recv()
        zs[h] = values[part(0, 1 - zl), :] + ar[h, 1 - zl, 0] + ar[h, 1 - zl, 1]
        pair = send(zs.at[h], zr.at[h], z_pair)
        mine = values[part(0, zl), :] + ar[h, zl, 0] + ar[h, zl, 1]
        top, bottom = obsv[0], obsv[1]
        low = lane_low((128, 128))
        if h == 0:
            mine -= jnp.where(low, top, swap_lanes(bottom))
        else:
            mine -= jnp.where(low, swap_lanes(top), bottom)
        zs2 = resp.at[h, 0]
        zs2[part(0, zl), :] = mine
        yield 8.5
        pair.wait_recv()
        zs2[part(0, zl), :] += zr[h]

        def share(at, sub, first, size, to):
            start = ((y + at) % 4) * 256 + sub * 128 + first
            rows = ds(start, size, 64)
            return send(zs2.at[rows], zs2.at[rows], to)

        up1 = share(0, zl, 0, 128, y_next)
        down1 = share(0, zl, 0, 128, y_prev)
        pair = share(0, zl, 0, 128, z_pair)
        yield 11.3
        up1.wait_recv()
        up2 = share(3, zl, 0, 64, y_next)
        down1.wait_recv()
        down2 = share(1, zl, 64, 64, y_prev)
        pair.wait_recv()
        up3 = share(0, 1 - zl, 0, 128, y_next)
        down3 = share(0, 1 - zl, 0, 128, y_prev)
        yield 14.0
        up3.wait_recv()
        up4 = share(3, 1 - zl, 0, 64, y_next)
        down3.wait_recv()
        down4 = share(1, 1 - zl, 64, 64, y_prev)
        yield 16.0
        for copy in (up2, down2, up4, down4):
            copy.wait_recv()

        half = zs2[...].astype(BF16)
        low = lane_low((64, 128))
        acc = []
        for i in range(2):
            acc.append(jnp.dot(xyt[pl.ds(i * 256, 256), :], half, preferred_element_type=F32))
        total = acc[0] + swap_lanes(acc[1])
        turned = swap_lanes(total)
        bsend[h] = jnp.where(low, total[128:192], turned[192:256])
        swap = send(bsend.at[h], brecv.at[h], sibling)
        mine = jnp.where(low, total[0:64], turned[64:128])
        copies = [send(zs2, resp.at[h, 1], sibling)]
        yield 18.5
        swap.wait_recv()
        k_index = lax.broadcasted_iota(jnp.int32, (64, 128), 0) + jnp.where(low, 0, 64)
        mine = jnp.where(k_index < rank[0, 0], mine + brecv[h], 0.0)
        bx[h, 0] = mine.astype(BF16).astype(F32)
        copies += [
            send(bx.at[h, 0], bx.at[h, 1], x_prev),
            send(bx.at[h, 0], bx.at[h, 2], x_far),
            send(bx.at[h, 0], bx.at[h, 3], x_next),
        ]
        yield 21.5
        for copy in copies[1:]:
            copy.wait_recv()
        for d in range(4):
            packed = bx[h, d]
            turned = swap_lanes(packed)
            bd[h, pl.ds(d * 256, 64), :] = jnp.where(low, packed, 0.0).astype(BF16)
            bd[h, pl.ds(d * 256 + 64, 64), :] = jnp.where(low, turned, 0.0).astype(BF16)
            bd[h, pl.ds(d * 256 + 128, 64), :] = jnp.where(low, 0.0, turned).astype(BF16)
            bd[h, pl.ds(d * 256 + 192, 64), :] = jnp.where(low, 0.0, packed).astype(BF16)

        part_grad = grad.at[h]

        def gradient(i, carry):
            rows = ds(i * 256, 256, 256)
            part_grad[rows, :] = jnp.dot(grcat[rows, :], bd[h], preferred_element_type=F32)
            return carry

        lax.fori_loop(0, 2, gradient, 0)

        def piece(at, sub):
            return ds(((zh + at) % 4) * 128 + sub * 64, 64, 64)

        up1 = send(part_grad.at[piece(2, 0)], cm1.at[h, 0], zh_next)
        down1 = send(part_grad.at[piece(2, 1)], cm1.at[h, 1], zh_prev)
        up2 = send(part_grad.at[piece(1, 1)], cr.at[h, 1, 0], zh_next)
        down2 = send(part_grad.at[piece(3, 0)], cr.at[h, 0, 1], zh_prev)
        yield 25.0
        up1.wait_recv()
        cm3[h, 0] = part_grad[piece(1, 0), :] + cm1[h, 0]
        up3 = send(cm3.at[h, 0], cr.at[h, 0, 0], zh_next)
        down1.wait_recv()
        cm3[h, 1] = part_grad[piece(3, 1), :] + cm1[h, 1]
        down3 = send(cm3.at[h, 1], cr.at[h, 1, 1], zh_prev)
        yield 28.0
        for copy in (up2, down2, up3, down3):
            copy.wait_recv()
        final = outp.at[h]
        for sub in range(2):
            total = part_grad[piece(0, sub), :] + cr[h, sub, 0] + cr[h, sub, 1]
            rows = ds(row * 128 + sub * 64, 64, 64)
            final[rows, :] = jnp.maximum(base[h, pl.ds(sub * 64, 64), :] - 0.5 * total, 0.0)

        def spread(x_at, zh_at, first, size, to):
            start = (((x + x_at) % 4) * 4 + (zh + zh_at) % 4) * 128 + first
            rows = ds(start, size, 64)
            return send(final.at[rows], final.at[rows], to)

        z_up1 = spread(0, 0, 0, 128, zh_next)
        z_down1 = spread(0, 0, 0, 128, zh_prev)
        x_up, x_down, last = {}, {}, []
        x_up[0] = spread(0, 0, 0, 128, x_next)
        x_down[0] = spread(0, 0, 0, 128, x_prev)

        def pass_on(at):
            x_up[at].wait_recv()
            last.append(spread(3, at, 0, 64, x_next))
            x_down[at].wait_recv()
            last.append(spread(1, at, 64, 64, x_prev))

        yield 32.5
        z_up1.wait_recv()
        z_up2 = spread(0, 3, 0, 64, zh_next)
        x_up[3] = spread(0, 3, 0, 128, x_next)
        x_down[3] = spread(0, 3, 0, 128, x_prev)
        z_down1.wait_recv()
        z_down2 = spread(0, 1, 64, 64, zh_prev)
        x_up[1] = spread(0, 1, 0, 128, x_next)
        x_down[1] = spread(0, 1, 0, 128, x_prev)
        pass_on(0)
        yield 36.0
        z_up2.wait_recv()
        z_down2.wait_recv()
        x_up[2] = spread(0, 2, 0, 128, x_next)
        x_down[2] = spread(0, 2, 0, 128, x_prev)
        pass_on(3)
        yield 37.5
        pass_on(1)
        yield 39.0
        pass_on(2)
        yield 41.0
        for copy in last:
            copy.wait_recv()
        copies[0].wait_recv()

    def side():
        yield 0.1

        def turn(i, carry):
            rows = ds(i * 128, 128, 128)
            for j in range(4):
                xyt[pl.ds(j * 128, 128), rows] = xy[rows, pl.ds(j * 128, 128)].T
            return carry

        lax.fori_loop(0, 8, turn, 0)
        yield 7.5
        load_nbr.wait()
        for copy in halo:
            copy.wait_recv()
        first = col * 2048 + row * 128 - HALO
        place = lax.broadcasted_iota(jnp.int32, (256, 128), 0) + first
        links = jnp.zeros((256, 128), F32)
        for index in range(8):
            links += (nbrv[pl.ds(index, 1), :] == place).astype(F32)
        links = links.astype(BF16)
        window = ext[ds(row * 128, 256, 128), :]
        high = window.astype(BF16)
        rest = (window - high.astype(F32)).astype(BF16)
        dims = (((0,), (0,)), ((), ()))
        near = lax.dot_general(links, high, dims, preferred_element_type=F32)
        near += lax.dot_general(links, rest, dims, preferred_element_type=F32)
        own = ext[ds(row * 128 + HALO, 128, 64), :]
        wide = own - 0.025 * (8.0 * own - near)
        left, right = wide[:, :128], wide[:, 128:]
        low = lane_low((128, 128))
        base[0] = jnp.where(low, left, swap_lanes(right))
        base[1] = jnp.where(low, swap_lanes(left), right)
        grcat[:, pl.ds(0, 256)] = grv[x_block(0), :]
        yield 20.9
        for d in range(1, 4):
            share_gr[d - 1].wait_recv()
            grcat[:, pl.ds(d * 256, 256)] = grrecv[d - 1].astype(BF16)

    tasks = [(0.0, 0, chain(0)), (0.05, 1, chain(1)), (0.06, 2, side())]
    shift = {0: 0.0, 1: 3.9, 2: 0.0}
    while tasks:
        tasks.sort(key=lambda task: task[:2])
        _, number, task = tasks.pop(0)
        at = next(task, None)
        if at is not None:
            tasks.append((at + shift[number], number, task))

    def join_res(i, carry):
        low = lane_low((128, 128))
        rows = ds(i * 128, 128, 128)
        for half in range(2):
            first, second = resp[0, half, rows, :], resp[1, half, rows, :]
            at = (k if half == 0 else 1 - k) * 2048 + i * 128
            resv[ds(at, 128, 128), :] = jnp.where(low, first, swap_lanes(second))
            resv[ds(at + 1024, 128, 128), :] = jnp.where(low, swap_lanes(first), second)
        return carry

    lax.fori_loop(0, 8, join_res, 0)
    store_res = local(resv, res)

    def join_out(i, carry):
        low = lane_low((128, 128))
        rows = ds(i * 128, 128, 128)
        first, second = outp[0, rows, :], outp[1, rows, :]
        outv[rows, pl.ds(0, 128)] = jnp.where(low, first, swap_lanes(second))
        outv[rows, pl.ds(128, 128)] = jnp.where(low, swap_lanes(first), second)
        return carry

    lax.fori_loop(0, 16, join_out, 0)
    store_out = local(outv, out)
    for copy in sends:
        copy.wait_send()
    store_res.wait()
    store_out.wait()


def body(observed, slip, green_left, green_right, block_ranks, neighbours):
    vmem, dma = pltpu.VMEM, pltpu.SemaphoreType.DMA
    hbm = pl.BlockSpec(memory_space=pl.ANY)
    return pl.pallas_call(
        kernel,
        name="step",
        out_shape=(
            jax.ShapeDtypeStruct((2048, 256), F32),
            jax.ShapeDtypeStruct((4096, 128), F32),
        ),
        in_specs=[hbm, hbm, hbm, hbm, pl.BlockSpec(memory_space=pltpu.SMEM), hbm],
        out_specs=(hbm, hbm),
        scratch_shapes=[
            vmem((2048 + 2 * HALO, 256), F32),
            vmem((4096, 128), BF16),
            vmem((2048, 256), BF16),
            vmem((2, 128, 128), F32),
            vmem((8, 128), jnp.int32),
            vmem((2048, 128), F32),
            vmem((2048, 128), F32),
            vmem((1024, 512), BF16),
            vmem((512, 1024), BF16),
            vmem((2048, 256), F32),
            vmem((3, 512, 256), F32),
            vmem((512, 1024), BF16),
            vmem((128, 128), F32),
            vmem((128, 128), F32),
            vmem((2, 512, 128), BF16),
            vmem((2, 1024, 128), F32),
            vmem((2, 2, 128, 128), F32),
            vmem((2, 2, 2, 128, 128), F32),
            vmem((2, 2, 128, 128), F32),
            vmem((2, 128, 128), F32),
            vmem((2, 128, 128), F32),
            vmem((2, 2, 1024, 128), F32),
            vmem((2, 64, 128), F32),
            vmem((2, 64, 128), F32),
            vmem((2, 4, 64, 128), F32),
            vmem((2, 1024, 128), BF16),
            vmem((2, 512, 128), F32),
            vmem((2, 2, 64, 128), F32),
            vmem((2, 2, 2, 64, 128), F32),
            vmem((2, 2, 64, 128), F32),
            vmem((2, 128, 128), F32),
            vmem((2, 2048, 128), F32),
            vmem((2048, 256), F32),
            vmem((4096, 128), F32),
            dma((N_SEM,)),
            dma((N_SEM,)),
            dma((32,)),
        ],
        compiler_params=pltpu.CompilerParams(
            collective_id=0, has_side_effects=True, vmem_limit_bytes=48 * 2**20
        ),
        cost_estimate=pl.CostEstimate(flops=10**9, bytes_accessed=12 * 2**20, transcendentals=0),
    )(observed, slip, green_left, green_right, block_ranks, neighbours.T)


def solution(mesh):
    return jax.shard_map(
        body,
        mesh=mesh,
        in_specs=(
            P("row", None),
            P("col", None),
            P("row", "col"),
            P("col", "row"),
            P("row", "col"),
            P("col", None),
        ),
        out_specs=(P("col", None), P("row", None)),
        check_vma=False,
    )
```

```python
import jax
import jax.numpy as jnp
from jax import lax
from jax.experimental import pallas as pl
from jax.experimental.pallas import tpu as pltpu
from jax.sharding import PartitionSpec as P

MESH = pl.DeviceIdType.MESH
F32 = jnp.float32
BF16 = jnp.bfloat16
HALO = 64
N_SEM = 160


def lane_low(shape):
    return lax.broadcasted_iota(jnp.int32, shape, 1) < 64


def swap_lanes(value):
    return pltpu.roll(value, 64, 1)


def ds(start, size, unit):
    if isinstance(start, int):
        return pl.ds(start, size)
    return pl.ds(pl.multiple_of(start, unit), size)


def kernel(
    obs, slip, gl, gr, rank, nbr, out, res,
    ext, glv, grv, obsv, nbrv, glsend, glrecv, xy, xyt, grsend, grrecv, grcat,
    insend, inrecv, rhs, pred, azr, azs, ay, af, afs, resp, bsend, brecv, bx, bd, grad,
    cm1, cr, cm3, base, outp, send_sem, recv_sem, local_sem,
):
    row = lax.axis_index("row")
    col = lax.axis_index("col")
    x, zh = row // 4, row % 4
    zl, y, k = col // 8, (col // 2) % 4, col % 2

    def device(x, zh, zl, y, k):
        return (x * 4 + zh, (zl * 4 + y) * 2 + k)

    sibling = device(x, zh, zl, y, 1 - k)
    y_next = device(x, zh, zl, (y + 1) % 4, k)
    y_prev = device(x, zh, zl, (y + 3) % 4, k)
    y_far = device(x, zh, zl, (y + 2) % 4, k)
    z_pair = device(x, zh, 1 - zl, y, k)
    x_next = device((x + 1) % 4, zh, zl, y, k)
    x_prev = device((x + 3) % 4, zh, zl, y, k)
    x_far = device((x + 2) % 4, zh, zl, y, k)
    zh_next = device(x, (zh + 1) % 4, zl, y, k)
    zh_prev = device(x, (zh + 3) % 4, zl, y, k)
    col_next = (row, (col + 1) % 16)
    col_prev = (row, (col + 15) % 16)

    counts = [0, 0]
    sends = []

    def send(src, dst, to):
        index = counts[0]
        counts[0] += 1
        copy = pltpu.make_async_remote_copy(
            src_ref=src, dst_ref=dst, send_sem=send_sem.at[index], recv_sem=recv_sem.at[index],
            device_id=to, device_id_type=MESH,
        )
        copy.start()
        sends.append(copy)
        return copy

    def local(src, dst):
        index = counts[1]
        counts[1] += 1
        copy = pltpu.make_async_copy(src, dst, local_sem.at[index])
        copy.start()
        return copy

    partners = (
        sibling, col_next, col_prev, zh_next, zh_prev, x_next, x_prev, x_far, y_next, y_prev, y_far, z_pair,
    )

    load_gl = [
        local(gl.at[ds((1 - k) * 2048, 2048, 2048)], glv.at[pl.ds(2048, 2048)]),
    ]
    load_gr, load_slip = [], []
    for piece in range(4):
        rows = pl.ds(piece * 512, 512)
        load_gr.append(local(gr.at[rows], grv.at[rows]))
        load_slip.append(local(slip.at[rows], ext.at[pl.ds(HALO + piece * 512, 512)]))
    load_gl.append(local(gl.at[ds(k * 2048, 2048, 2048)], glv.at[pl.ds(0, 2048)]))
    shard = y * 256 + zl * 128
    load_obs = [
        local(obs.at[ds(k * 2048 + half * 1024 + shard, 128, 128)], obsv.at[half]) for half in range(2)
    ]
    load_nbr = local(nbr.at[:, ds(row * 128, 128, 128)], nbrv)

    barrier = pltpu.get_barrier_semaphore()
    for partner in partners:
        pl.semaphore_signal(barrier, inc=1, device_id=partner, device_id_type=MESH)

    keep = lax.broadcasted_iota(jnp.int32, (128, 128), 0) < rank[0, 0]
    keep_lane = lax.broadcasted_iota(jnp.int32, (256, 128), 1) < rank[0, 0]
    early = {}

    def x_block(at):
        return ds(((x + at) % 4) * 512, 512, 512)

    def start():
        load_gl[0].wait()

        def widen_left(i, carry):
            rows = ds(i * 256, 256, 256)
            left = glv[ds(2048 + i * 256, 256, 256), :].astype(F32)
            glsend[rows, :] = jnp.where(keep_lane, left, 0.0)
            return carry

        lax.fori_loop(0, 8, widen_left, 0)
        yield -9.0
        pl.semaphore_wait(barrier, len(partners))
        swap_gl = [
            send(glsend.at[pl.ds(i * 512, 512)], glrecv.at[pl.ds(i * 512, 512)], sibling) for i in range(4)
        ]
        yield -8.0
        inner = jnp.zeros((128, 128), F32)
        for piece in range(4):
            load_gr[piece].wait()
            load_slip[piece].wait()
            for rake in range(2):
                lanes = pl.ds(rake * 128, 128)
                inner += lax.dot_general(
                    grv[pl.ds(piece * 512, 512), lanes],
                    ext[pl.ds(HALO + piece * 512, 512), lanes].astype(BF16),
                    (((0,), (0,)), ((), ())),
                    preferred_element_type=F32,
                )
        inner = jnp.where(keep, inner, 0.0).astype(BF16).astype(F32)
        insend[...] = inner
        swap_inner = send(insend, inrecv, sibling)
        yield -7.0

        def widen_right(i, carry):
            rows = ds(i * 256, 256, 256)
            grsend[rows, :] = grv[rows, :].astype(F32)
            return carry

        lax.fori_loop(0, 8, widen_right, 0)
        early["gr"] = [
            send(grsend.at[x_block(3)], grrecv.at[0], x_prev),
            send(grsend.at[x_block(2)], grrecv.at[1], x_far),
            send(grsend.at[x_block(1)], grrecv.at[2], x_next),
        ]
        early["halo"] = [
            send(ext.at[pl.ds(2048, HALO)], ext.at[pl.ds(0, HALO)], col_next),
            send(ext.at[pl.ds(HALO, HALO)], ext.at[pl.ds(2048 + HALO, HALO)], col_prev),
        ]
        yield -6.0
        load_gl[1].wait()

        def own_left(i, carry):
            rows = ds(i * 256, 256, 256)
            for half in range(2):
                left = glv[ds(half * 1024 + i * 256, 256, 256), :].astype(F32)
                xy[rows, pl.ds(half * 256, 128)] = jnp.where(keep_lane, left, 0.0).astype(BF16)
            return carry

        lax.fori_loop(0, 4, own_left, 0)
        yield -5.0
        for copy in swap_gl:
            copy.wait_recv()

        def other_left(i, carry):
            rows = ds(i * 256, 256, 256)
            for half in range(2):
                xy[rows, pl.ds(half * 256 + 128, 128)] = glrecv[ds(half * 1024 + i * 256, 256, 256), :].astype(BF16)
            return carry

        lax.fori_loop(0, 4, other_left, 0)
        yield -4.0
        for copy in load_obs:
            copy.wait()
        swap_inner.wait_recv()
        low = lane_low((256, 128))
        both = jnp.concatenate([inner, inrecv[...]], axis=0)
        turned = swap_lanes(both)
        rhs[0, pl.ds(0, 256), :] = jnp.where(low, both, 0.0).astype(BF16)
        rhs[0, pl.ds(256, 256), :] = jnp.where(low, 0.0, turned).astype(BF16)
        rhs[1, pl.ds(0, 256), :] = jnp.where(low, turned, 0.0).astype(BF16)
        rhs[1, pl.ds(256, 256), :] = jnp.where(low, 0.0, both).astype(BF16)
        yield -3.0

    def chain(h):
        lag = 4.0 * h
        if h == 1:
            yield 2.0
        values = pred.at[h]

        def predict(i, carry):
            rows = ds(i * 256, 256, 256)
            values[rows, :] = jnp.dot(xy[rows, :], rhs[h], preferred_element_type=F32)
            return carry

        lax.fori_loop(0, 4, predict, 0)

        def part(at, sub):
            return ds(((y + at) % 4) * 256 + sub * 128, 128, 128)

        other = 1 - zl
        pair1 = send(values.at[part(2, other)], azr.at[h, 0], z_pair)
        up1 = send(values.at[part(1, other)], ay.at[h, 0], y_next)
        down1 = send(values.at[part(3, other)], ay.at[h, 1], y_prev)
        up2 = send(values.at[part(1, zl)], af.at[h, 0], y_next)
        down2 = send(values.at[part(3, zl)], af.at[h, 1], y_prev)
        yield 3.6 + lag
        up1.wait_recv()
        down1.wait_recv()
        azs[h] = values[part(0, other), :] + ay[h, 0] + ay[h, 1]
        pair2 = send(azs.at[h], azr.at[h, 1], z_pair)
        pair1.wait_recv()
        afs[h] = values[part(2, zl), :] + azr[h, 0]
        far = send(afs.at[h], af.at[h, 2], y_far)
        top, bottom = obsv[0], obsv[1]
        low = lane_low((128, 128))
        if h == 0:
            seen = jnp.where(low, top, swap_lanes(bottom))
        else:
            seen = jnp.where(low, swap_lanes(top), bottom)
        residual = resp.at[h, 0]
        residual[part(0, zl), :] = values[part(0, zl), :] - seen
        yield 8.0 + lag
        for copy in (up2, down2, pair2, far):
            copy.wait_recv()
        mine = residual.at[part(0, zl)]
        mine[...] = mine[...] + af[h, 0] + af[h, 1] + af[h, 2] + azr[h, 1]

        def share(at, sub, to):
            shard = residual.at[part(at, sub)]
            return send(shard, shard, to)

        pair1 = share(0, zl, z_pair)
        far = share(0, zl, y_far)
        up1 = share(0, zl, y_next)
        down1 = share(0, zl, y_prev)
        yield 11.8 + lag
        pair1.wait_recv()
        up2 = share(0, other, y_next)
        down2 = share(0, other, y_prev)
        yield 13.0 + lag
        far.wait_recv()
        pair2 = share(2, zl, z_pair)
        yield 16.8 + lag
        for copy in (up1, down1, up2, down2, pair2):
            copy.wait_recv()

        half = residual[...].astype(BF16)
        low = lane_low((64, 128))
        acc = []
        for i in range(2):
            acc.append(jnp.dot(xyt[pl.ds(i * 256, 256), :], half, preferred_element_type=F32))
        total = acc[0] + swap_lanes(acc[1])
        turned = swap_lanes(total)
        bsend[h] = jnp.where(low, total[128:192], turned[192:256])
        swap = send(bsend.at[h], brecv.at[h], sibling)
        mine = jnp.where(low, total[0:64], turned[64:128])
        yield 18.0 + lag
        swap.wait_recv()
        bx[h, 0] = (mine + brecv[h]).astype(BF16).astype(F32)
        shares = [
            send(bx.at[h, 0], bx.at[h, 2], x_far),
            send(bx.at[h, 0], bx.at[h, 1], x_prev),
            send(bx.at[h, 0], bx.at[h, 3], x_next),
        ]
        early[h] = send(residual, resp.at[h, 1], sibling)
        yield 22.0 + lag
        for copy in shares:
            copy.wait_recv()
        for d in range(4):
            packed = bx[h, d]
            turned = swap_lanes(packed)
            bd[h, pl.ds(d * 256, 64), :] = jnp.where(low, packed, 0.0).astype(BF16)
            bd[h, pl.ds(d * 256 + 64, 64), :] = jnp.where(low, turned, 0.0).astype(BF16)
            bd[h, pl.ds(d * 256 + 128, 64), :] = jnp.where(low, 0.0, turned).astype(BF16)
            bd[h, pl.ds(d * 256 + 192, 64), :] = jnp.where(low, 0.0, packed).astype(BF16)

        part_grad = grad.at[h]

        def gradient(i, carry):
            rows = ds(i * 256, 256, 256)
            part_grad[rows, :] = jnp.dot(grcat[rows, :], bd[h], preferred_element_type=F32)
            return carry

        lax.fori_loop(0, 2, gradient, 0)

        def piece(at, sub):
            return ds(((zh + at) % 4) * 128 + sub * 64, 64, 64)

        up1 = send(part_grad.at[piece(2, 0)], cm1.at[h, 0], zh_next)
        down1 = send(part_grad.at[piece(2, 1)], cm1.at[h, 1], zh_prev)
        up2 = send(part_grad.at[piece(1, 1)], cr.at[h, 1, 0], zh_next)
        down2 = send(part_grad.at[piece(3, 0)], cr.at[h, 0, 1], zh_prev)
        yield 27.0 + lag
        up1.wait_recv()
        cm3[h, 0] = part_grad[piece(1, 0), :] + cm1[h, 0]
        up3 = send(cm3.at[h, 0], cr.at[h, 0, 0], zh_next)
        down1.wait_recv()
        cm3[h, 1] = part_grad[piece(3, 1), :] + cm1[h, 1]
        down3 = send(cm3.at[h, 1], cr.at[h, 1, 1], zh_prev)
        yield 31.3 + lag
        for copy in (up2, down2, up3, down3):
            copy.wait_recv()
        final = outp.at[h]
        for sub in range(2):
            total = part_grad[piece(0, sub), :] + cr[h, sub, 0] + cr[h, sub, 1]
            rows = ds(row * 128 + sub * 64, 64, 64)
            final[rows, :] = jnp.maximum(base[h, pl.ds(sub * 64, 64), :] - 0.5 * total, 0.0)

        def spread(x_at, zh_at, first, size, to):
            start = (((x + x_at) % 4) * 4 + (zh + zh_at) % 4) * 128 + first
            rows = ds(start, size, 64)
            return send(final.at[rows], final.at[rows], to)

        z_up1 = spread(0, 0, 0, 128, zh_next)
        z_down1 = spread(0, 0, 0, 128, zh_prev)
        x_up, x_down, last = {}, {}, {}
        x_up[0] = spread(0, 0, 0, 128, x_next)
        x_down[0] = spread(0, 0, 0, 128, x_prev)

        def pass_on(at):
            x_up[at].wait_recv()
            copies = [spread(3, at, 0, 64, x_next)]
            x_down[at].wait_recv()
            copies.append(spread(1, at, 64, 64, x_prev))
            last[at] = copies
            if h == 1:
                join(3, at)
                join(1, at)

        def finish(at):
            for copy in last[at]:
                copy.wait_recv()
            if h == 1:
                join(2, at)

        yield 35.2 + lag
        if h == 1:
            join(0, 0)
        pass_on(0)
        yield 37.2 + lag
        z_up1.wait_recv()
        z_up2 = spread(0, 3, 0, 64, zh_next)
        x_up[3] = spread(0, 3, 0, 128, x_next)
        x_down[3] = spread(0, 3, 0, 128, x_prev)
        z_down1.wait_recv()
        z_down2 = spread(0, 1, 64, 64, zh_prev)
        x_up[1] = spread(0, 1, 0, 128, x_next)
        x_down[1] = spread(0, 1, 0, 128, x_prev)
        if h == 1:
            join(0, 3)
            join(0, 1)
        yield 41.3 + lag
        z_up2.wait_recv()
        z_down2.wait_recv()
        x_up[2] = spread(0, 2, 0, 128, x_next)
        x_down[2] = spread(0, 2, 0, 128, x_prev)
        if h == 1:
            x_last = spread(0, 2, 0, 128, x_far)
            join(0, 2)
        finish(0)
        yield 41.6 + lag
        pass_on(3)
        yield 41.7 + lag
        pass_on(1)
        yield 45.0 + lag
        if h == 0:
            pass_on(2)
        else:
            x_up[2].wait_recv()
            join(3, 2)
            x_down[2].wait_recv()
            join(1, 2)
        finish(3)
        finish(1)
        yield 47.0 + lag
        if h == 0:
            finish(2)
        else:
            x_last.wait_recv()
            join(2, 2)

    def join(x_at, zh_at):
        low = lane_low((128, 128))
        rows = ds((((x + x_at) % 4) * 4 + (zh + zh_at) % 4) * 128, 128, 128)
        first, second = outp[0, rows, :], outp[1, rows, :]
        out[rows, pl.ds(0, 128)] = jnp.where(low, first, swap_lanes(second))
        out[rows, pl.ds(128, 128)] = jnp.where(low, swap_lanes(first), second)

    def join_res(half):
        def join_rows(i, carry):
            low = lane_low((128, 128))
            rows = ds(i * 128, 128, 128)
            first, second = resp[0, half, rows, :], resp[1, half, rows, :]
            at = (k if half == 0 else 1 - k) * 2048 + i * 128
            res[ds(at, 128, 128), :] = jnp.where(low, first, swap_lanes(second))
            res[ds(at + 1024, 128, 128), :] = jnp.where(low, swap_lanes(first), second)
            return carry

        lax.fori_loop(0, 8, join_rows, 0)

    def side():
        yield 0.1

        def turn(i, carry):
            rows = ds(i * 128, 128, 128)
            for j in range(4):
                xyt[pl.ds(j * 128, 128), rows] = xy[rows, pl.ds(j * 128, 128)].T
            return carry

        lax.fori_loop(0, 8, turn, 0)
        yield 8.2
        load_nbr.wait()
        for copy in early["halo"]:
            copy.wait_recv()
        first = col * 2048 + row * 128 - HALO
        place = lax.broadcasted_iota(jnp.int32, (256, 128), 0) + first
        links = jnp.zeros((256, 128), F32)
        for index in range(8):
            links += (nbrv[pl.ds(index, 1), :] == place).astype(F32)
        links = links.astype(BF16)
        window = ext[ds(row * 128, 256, 128), :]
        high = window.astype(BF16)
        rest = (window - high.astype(F32)).astype(BF16)
        dims = (((0,), (0,)), ((), ()))
        near = lax.dot_general(links, high, dims, preferred_element_type=F32)
        near += lax.dot_general(links, rest, dims, preferred_element_type=F32)
        own = ext[ds(row * 128 + HALO, 128, 64), :]
        wide = own - 0.025 * (8.0 * own - near)
        left, right = wide[:, :128], wide[:, 128:]
        low = lane_low((128, 128))
        base[0] = jnp.where(low, left, swap_lanes(right))
        base[1] = jnp.where(low, swap_lanes(left), right)
        grcat[:, pl.ds(0, 256)] = grv[x_block(0), :]
        yield 18.2
        for d in range(1, 4):
            early["gr"][d - 1].wait_recv()
            grcat[:, pl.ds(d * 256, 256)] = grrecv[d - 1].astype(BF16)

        yield 27.6
        join_res(0)
        yield 35.5
        for h in range(2):
            early[h].wait_recv()
        join_res(1)

    tasks = [(-10.0, 3, start())]
    while tasks:
        tasks.sort(key=lambda task: task[:2])
        _, number, task = tasks.pop(0)
        at = next(task, None)
        if at is not None:
            tasks.append((at, number, task))
        elif number == 3:
            tasks = [(0.0, 0, chain(0)), (0.05, 1, chain(1)), (0.06, 2, side())]
    for copy in sends:
        copy.wait_send()


def store(out_in, res_in, out, res, sem):
    copies = [
        pltpu.make_async_copy(out_in, out, sem.at[0]),
        pltpu.make_async_copy(res_in, res, sem.at[1]),
    ]
    for copy in copies:
        copy.start()
    for copy in copies:
        copy.wait()


def body(observed, slip, green_left, green_right, block_ranks, neighbours):
    vmem, dma = pltpu.VMEM, pltpu.SemaphoreType.DMA
    hbm = pl.BlockSpec(memory_space=pltpu.HBM)
    whole = pl.BlockSpec(memory_space=pltpu.VMEM)
    shapes = (
        jax.ShapeDtypeStruct((2048, 256), F32),
        jax.ShapeDtypeStruct((4096, 128), F32),
    )
    joined = pl.pallas_call(
        kernel,
        name="step",
        out_shape=tuple(vmem(shape.shape, F32) for shape in shapes),
        in_specs=[hbm, hbm, hbm, hbm, pl.BlockSpec(memory_space=pltpu.SMEM), hbm],
        out_specs=(whole, whole),
        scratch_shapes=[
            vmem((2048 + 2 * HALO, 256), F32),
            vmem((4096, 128), BF16),
            vmem((2048, 256), BF16),
            vmem((2, 128, 128), F32),
            vmem((8, 128), jnp.int32),
            vmem((2048, 128), F32),
            vmem((2048, 128), F32),
            vmem((1024, 512), BF16),
            vmem((512, 1024), BF16),
            vmem((2048, 256), F32),
            vmem((3, 512, 256), F32),
            vmem((512, 1024), BF16),
            vmem((128, 128), F32),
            vmem((128, 128), F32),
            vmem((2, 512, 128), BF16),
            vmem((2, 1024, 128), F32),
            vmem((2, 2, 128, 128), F32),
            vmem((2, 128, 128), F32),
            vmem((2, 2, 128, 128), F32),
            vmem((2, 3, 128, 128), F32),
            vmem((2, 128, 128), F32),
            vmem((2, 2, 1024, 128), F32),
            vmem((2, 64, 128), F32),
            vmem((2, 64, 128), F32),
            vmem((2, 4, 64, 128), F32),
            vmem((2, 1024, 128), BF16),
            vmem((2, 512, 128), F32),
            vmem((2, 2, 64, 128), F32),
            vmem((2, 2, 2, 64, 128), F32),
            vmem((2, 2, 64, 128), F32),
            vmem((2, 128, 128), F32),
            vmem((2, 2048, 128), F32),
            dma((N_SEM,)),
            dma((N_SEM,)),
            dma((32,)),
        ],
        compiler_params=pltpu.CompilerParams(
            collective_id=0, has_side_effects=True, vmem_limit_bytes=40 * 2**20
        ),
        cost_estimate=pl.CostEstimate(flops=10**9, bytes_accessed=12 * 2**20, transcendentals=0),
    )(*(pltpu.with_memory_space_constraint(value, pltpu.HBM) for value in (observed, slip, green_left, green_right)), block_ranks, pltpu.with_memory_space_constraint(neighbours.T, pltpu.HBM))
    return pl.pallas_call(
        store,
        name="store",
        out_shape=shapes,
        in_specs=[whole, whole],
        out_specs=(hbm, hbm),
        scratch_shapes=[dma((2,))],
    )(*joined)


def solution(mesh):
    return jax.shard_map(
        body,
        mesh=mesh,
        in_specs=(
            P("row", None),
            P("col", None),
            P("row", "col"),
            P("col", "row"),
            P("row", "col"),
            P("col", None),
        ),
        out_specs=(P("col", None), P("row", None)),
        check_vma=False,
    )
```

```python
import jax
import jax.numpy as jnp
from jax import lax
from jax.experimental import pallas as pl
from jax.experimental.pallas import tpu as pltpu
from jax.sharding import PartitionSpec as P

MESH = pl.DeviceIdType.MESH
F32 = jnp.float32
BF16 = jnp.bfloat16
HALO = 64
N_SEM = 240
LAG_FORWARD, LAG_BACK = 3.5, 5.0
FAR_OVER_Z = ((0, 0), (0, 1), (1, 0), (1, 1))


def lane_low(shape):
    return lax.broadcasted_iota(jnp.int32, shape, 1) < 64


def swap_lanes(value):
    return pltpu.roll(value, 64, 1)


def ds(start, size, unit):
    if isinstance(start, int):
        return pl.ds(start, size)
    return pl.ds(pl.multiple_of(start, unit), size)


def kernel(
    obs, slip, gl, gr, rank, nbr, out, res,
    ext, glv, grv, obsv, nbrv, glsend, glrecv, xy, grsend, grrecv, grcat,
    rhs, pred, psend, precv, azr, azs, ay, af, afs, resp, bsend, brecv, bx, bd, grad,
    cm1, cr, cm3, base, outp, send_sem, recv_sem, local_sem,
):
    row = lax.axis_index("row")
    col = lax.axis_index("col")
    x, zh = row // 4, row % 4
    zl, y, k = col // 8, (col // 2) % 4, col % 2

    def device(x, zh, zl, y, k):
        return (x * 4 + zh, (zl * 4 + y) * 2 + k)

    sibling = device(x, zh, zl, y, 1 - k)
    y_next = device(x, zh, zl, (y + 1) % 4, k)
    y_prev = device(x, zh, zl, (y + 3) % 4, k)
    y_far = device(x, zh, zl, (y + 2) % 4, k)
    z_pair = device(x, zh, 1 - zl, y, k)
    x_next = device((x + 1) % 4, zh, zl, y, k)
    x_prev = device((x + 3) % 4, zh, zl, y, k)
    x_far = device((x + 2) % 4, zh, zl, y, k)
    zh_next = device(x, (zh + 1) % 4, zl, y, k)
    zh_prev = device(x, (zh + 3) % 4, zl, y, k)
    col_next = (row, (col + 1) % 16)
    col_prev = (row, (col + 15) % 16)

    counts = [0, 0]
    sends = []

    def send(src, dst, to):
        index = counts[0]
        counts[0] += 1
        copy = pltpu.make_async_remote_copy(
            src_ref=src, dst_ref=dst, send_sem=send_sem.at[index], recv_sem=recv_sem.at[index],
            device_id=to, device_id_type=MESH,
        )
        copy.start()
        sends.append(copy)
        return copy

    def local(src, dst):
        index = counts[1]
        counts[1] += 1
        copy = pltpu.make_async_copy(src, dst, local_sem.at[index])
        copy.start()
        return copy

    partners = (
        sibling, col_next, col_prev, zh_next, zh_prev, x_next, x_prev, x_far, y_next, y_prev, y_far, z_pair,
    )

    load_gr, load_slip = [], []
    for piece in range(4):
        rows = pl.ds(piece * 512, 512)
        load_gr.append(local(gr.at[rows], grv.at[rows]))
        load_slip.append(local(slip.at[rows], ext.at[pl.ds(HALO + piece * 512, 512)]))
    load_gl = [
        local(gl.at[ds((1 - k) * 2048, 2048, 2048)], glv.at[pl.ds(2048, 2048)]),
        local(gl.at[ds(k * 2048, 2048, 2048)], glv.at[pl.ds(0, 2048)]),
    ]
    shard = y * 128 + zl * 64
    load_obs = [
        local(obs.at[ds(k * 2048 + half * 1024 + piece * 512 + shard, 64, 64)], obsv.at[half, piece])
        for half in range(2)
        for piece in range(2)
    ]
    load_nbr = local(nbr.at[:, ds(row * 128, 128, 128)], nbrv)

    barrier = pltpu.get_barrier_semaphore()
    for partner in partners:
        pl.semaphore_signal(barrier, inc=1, device_id=partner, device_id_type=MESH)

    keep = lax.broadcasted_iota(jnp.int32, (128, 128), 0) < rank[0, 0]
    keep_lane = lax.broadcasted_iota(jnp.int32, (256, 128), 1) < rank[0, 0]
    early = {}

    def x_block(at):
        return ds(((x + at) % 4) * 512, 512, 512)

    def product(half, h, s):
        first = half * 2048 + s * 512
        pair = jnp.concatenate([glv[pl.ds(first, 512), :], glv[pl.ds(first + 1024, 512), :]], axis=1)
        return jnp.dot(pair, rhs[h], preferred_element_type=F32)

    def start():
        inner = jnp.zeros((128, 128), F32)
        for piece in range(4):
            load_gr[piece].wait()
            load_slip[piece].wait()
            for rake in range(2):
                lanes = pl.ds(rake * 128, 128)
                inner += lax.dot_general(
                    grv[pl.ds(piece * 512, 512), lanes],
                    ext[pl.ds(HALO + piece * 512, 512), lanes].astype(BF16),
                    (((0,), (0,)), ((), ())),
                    preferred_element_type=F32,
                )
        inner = jnp.where(keep, inner, 0.0).astype(BF16).astype(F32)
        low = lane_low((128, 128))
        turned = swap_lanes(inner)
        rhs[0, pl.ds(0, 128), :] = jnp.where(low, inner, 0.0).astype(BF16)
        rhs[0, pl.ds(128, 128), :] = jnp.where(low, 0.0, turned).astype(BF16)
        rhs[1, pl.ds(0, 128), :] = jnp.where(low, turned, 0.0).astype(BF16)
        rhs[1, pl.ds(128, 128), :] = jnp.where(low, 0.0, inner).astype(BF16)
        load_gl[0].wait()
        for h in range(2):
            for s in range(2):
                psend[h, s] = product(1, h, s)
        def widen_right(i, carry):
            rows = ds(i * 256, 256, 256)
            grsend[rows, :] = grv[rows, :].astype(F32)
            return carry

        lax.fori_loop(0, 8, widen_right, 0)
        yield -9.0
        pl.semaphore_wait(barrier, len(partners))
        for h in range(2):
            for s in range(2):
                early["pred", h, s] = [
                    send(psend.at[h, s, pl.ds(i * 128, 128)], precv.at[h, s, pl.ds(i * 128, 128)], sibling)
                    for i in range(4)
                ]
        early["gr"] = [
            send(grsend.at[x_block(3)], grrecv.at[0], x_prev),
            send(grsend.at[x_block(2)], grrecv.at[1], x_far),
            send(grsend.at[x_block(1)], grrecv.at[2], x_next),
        ]
        yield -8.0
        load_gl[1].wait()
        for h in range(2):
            for s in range(2):
                pred[h, s] = product(0, h, s)
        yield -7.0
        for copy in load_obs:
            copy.wait()

    def prepare():
        yield 1.0

        def widen_left(i, carry):
            rows = ds(i * 256, 256, 256)
            left = glv[ds(2048 + i * 256, 256, 256), :].astype(F32)
            glsend[rows, :] = jnp.where(keep_lane, left, 0.0)
            return carry

        lax.fori_loop(0, 8, widen_left, 0)
        early["gl"] = [
            send(glsend.at[pl.ds(i * 512, 512)], glrecv.at[pl.ds(i * 512, 512)], sibling) for i in range(4)
        ]
        early["halo"] = [
            send(ext.at[pl.ds(2048, HALO)], ext.at[pl.ds(0, HALO)], col_next),
            send(ext.at[pl.ds(HALO, HALO)], ext.at[pl.ds(2048 + HALO, HALO)], col_prev),
        ]
        yield 4.5

        def own_left(i, carry):
            rows = ds(i * 256, 256, 256)
            for half in range(2):
                left = glv[ds(half * 1024 + i * 256, 256, 256), :].astype(F32)
                xy[rows, pl.ds(half * 256, 128)] = jnp.where(keep_lane, left, 0.0).astype(BF16)
            return carry

        lax.fori_loop(0, 4, own_left, 0)
        yield 9.0
        for copy in early["gl"]:
            copy.wait_recv()

        def other_left(i, carry):
            rows = ds(i * 256, 256, 256)
            for half in range(2):
                xy[rows, pl.ds(half * 256 + 128, 128)] = glrecv[ds(half * 1024 + i * 256, 256, 256), :].astype(BF16)
            return carry

        lax.fori_loop(0, 4, other_left, 0)

    def forward(h, s):
        lag = LAG_FORWARD * h + 0.8 * s
        if h == 1:
            yield 2.0 + 0.1 * s
        values = pred.at[h, s]
        for copy in early["pred", h, s]:
            copy.wait_recv()
        values[...] += precv[h, s]

        def part(at, sub):
            return ds(((y + at) % 4) * 128 + sub * 64, 64, 64)

        other = 1 - zl
        pair1 = send(values.at[part(2, other)], azr.at[h, s, 0], z_pair)
        up1 = send(values.at[part(1, other)], ay.at[h, s, 0], y_next)
        down1 = send(values.at[part(3, other)], ay.at[h, s, 1], y_prev)
        up2 = send(values.at[part(1, zl)], af.at[h, s, 0], y_next)
        down2 = send(values.at[part(3, zl)], af.at[h, s, 1], y_prev)
        yield 3.0 + lag
        up1.wait_recv()
        down1.wait_recv()
        azs[h, s] = values[part(0, other), :] + ay[h, s, 0] + ay[h, s, 1]
        pair2 = send(azs.at[h, s], azr.at[h, s, 1], z_pair)
        pair1.wait_recv()
        afs[h, s] = values[part(2, zl), :] + azr[h, s, 0]
        far = send(afs.at[h, s], af.at[h, s, 2], y_far)
        top, bottom = obsv[0, s], obsv[1, s]
        low = lane_low((64, 128))
        if h == 0:
            seen = jnp.where(low, top, swap_lanes(bottom))
        else:
            seen = jnp.where(low, swap_lanes(top), bottom)
        residual = resp.at[h, 0, pl.ds(s * 512, 512)]
        mine = residual.at[part(0, zl)]
        mine[...] = values[part(0, zl), :] - seen
        yield 6.8 + lag
        for copy in (up2, down2, pair2, far):
            copy.wait_recv()
        mine[...] = mine[...] + af[h, s, 0] + af[h, s, 1] + af[h, s, 2] + azr[h, s, 1]

        def share(at, sub, to):
            shard = residual.at[part(at, sub)]
            return send(shard, shard, to)

        pair1 = share(0, zl, z_pair)
        far = share(0, zl, y_far)
        up1 = share(0, zl, y_next)
        down1 = share(0, zl, y_prev)
        yield 9.9 + lag
        pair1.wait_recv()
        up2 = share(0, other, y_next)
        down2 = share(0, other, y_prev)
        yield 10.4 + lag
        far.wait_recv()
        pair2 = share(2, zl, z_pair)
        yield 13.6 + lag
        for copy in (up1, down1, up2, down2, pair2):
            copy.wait_recv()

    def backward(h):
        lag = LAG_BACK * h
        yield 14.5 + lag
        residual = resp.at[h, 0]
        low = lane_low((64, 128))
        acc = lax.dot_general(
            xy[...], residual[...].astype(BF16), (((0,), (0,)), ((), ())), preferred_element_type=F32
        )
        total = acc[:256] + swap_lanes(acc[256:])
        turned = swap_lanes(total)
        bsend[h] = jnp.where(low, total[128:192], turned[192:256])
        swap = send(bsend.at[h], brecv.at[h], sibling)
        mine = jnp.where(low, total[0:64], turned[64:128])
        yield 16.2 + lag
        swap.wait_recv()
        bx[h, 0] = (mine + brecv[h]).astype(BF16).astype(F32)
        shares = [
            send(bx.at[h, 0], bx.at[h, 2], x_far),
            send(bx.at[h, 0], bx.at[h, 1], x_prev),
            send(bx.at[h, 0], bx.at[h, 3], x_next),
        ]
        early[h] = send(residual, resp.at[h, 1], sibling)
        yield 19.6 + lag
        for copy in shares:
            copy.wait_recv()
        for d in range(4):
            packed = bx[h, d]
            turned = swap_lanes(packed)
            bd[h, pl.ds(d * 256, 64), :] = jnp.where(low, packed, 0.0).astype(BF16)
            bd[h, pl.ds(d * 256 + 64, 64), :] = jnp.where(low, turned, 0.0).astype(BF16)
            bd[h, pl.ds(d * 256 + 128, 64), :] = jnp.where(low, 0.0, turned).astype(BF16)
            bd[h, pl.ds(d * 256 + 192, 64), :] = jnp.where(low, 0.0, packed).astype(BF16)

    def update(h, s):
        lag = LAG_BACK * h + 0.8 * s
        yield 19.7 + LAG_BACK * h + 0.01 * s
        part_grad = grad.at[h, s]
        part_grad[...] = jnp.dot(grcat[pl.ds(s * 256, 256), :], bd[h], preferred_element_type=F32)

        def piece(at, sub):
            return ds(((zh + at) % 4) * 64 + sub * 32, 32, 32)

        up1 = send(part_grad.at[piece(2, 0)], cm1.at[h, s, 0], zh_next)
        down1 = send(part_grad.at[piece(2, 1)], cm1.at[h, s, 1], zh_prev)
        up2 = send(part_grad.at[piece(1, 1)], cr.at[h, s, 1, 0], zh_next)
        down2 = send(part_grad.at[piece(3, 0)], cr.at[h, s, 0, 1], zh_prev)
        yield 23.8 + lag
        up1.wait_recv()
        cm3[h, s, 0] = part_grad[piece(1, 0), :] + cm1[h, s, 0]
        up3 = send(cm3.at[h, s, 0], cr.at[h, s, 0, 0], zh_next)
        down1.wait_recv()
        cm3[h, s, 1] = part_grad[piece(3, 1), :] + cm1[h, s, 1]
        down3 = send(cm3.at[h, s, 1], cr.at[h, s, 1, 1], zh_prev)
        yield 27.6 + lag
        for copy in (up2, down2, up3, down3):
            copy.wait_recv()
        final = outp.at[h]
        for sub in range(2):
            total = part_grad[piece(0, sub), :] + cr[h, s, sub, 0] + cr[h, s, sub, 1]
            rows = ds(row * 128 + s * 64 + sub * 32, 32, 32)
            final[rows, :] = jnp.maximum(base[h, pl.ds(s * 64 + sub * 32, 32), :] - 0.5 * total, 0.0)

        def spread(x_at, zh_at, first, size, to):
            start = (((x + x_at) % 4) * 4 + (zh + zh_at) % 4) * 128 + s * 64 + first
            rows = ds(start, size, 32)
            return send(final.at[rows], final.at[rows], to)

        def merge(x_at, zh_at):
            if h == 1:
                join(x_at, zh_at, s)

        far_over_z = (h, s) in FAR_OVER_Z
        z_up1 = spread(0, 0, 0, 64, zh_next)
        z_down1 = spread(0, 0, 0, 64, zh_prev)
        x_up, x_down, last = {}, {}, {}
        x_up[0] = spread(0, 0, 0, 64, x_next)
        x_down[0] = spread(0, 0, 0, 64, x_prev)
        if far_over_z:
            far = spread(0, 0, 0, 64, x_far)

        def send_x(at):
            x_up[at] = spread(0, at, 0, 64, x_next)
            x_down[at] = spread(0, at, 0, 64, x_prev)

        def pass_on(at):
            x_up[at].wait_recv()
            if not far_over_z:
                last[at] = [spread(3, at, 0, 32, x_next)]
            x_down[at].wait_recv()
            if not far_over_z:
                last[at].append(spread(1, at, 32, 32, x_prev))
            merge(3, at)
            merge(1, at)

        def finish(at):
            for copy in last[at]:
                copy.wait_recv()
            merge(2, at)

        yield 30.7 + lag
        merge(0, 0)
        pass_on(0)
        yield 32.2 + lag
        z_up1.wait_recv()
        z_up2 = spread(0, 3, 0, 32, zh_next)
        z_down1.wait_recv()
        z_down2 = spread(0, 1, 32, 32, zh_prev)
        send_x(3)
        send_x(1)
        merge(0, 3)
        merge(0, 1)
        if far_over_z:
            yield 32.3 + lag
            far.wait_recv()
            z_up3 = spread(2, 0, 0, 64, zh_next)
            z_down3 = spread(2, 0, 0, 64, zh_prev)
            merge(2, 0)
        yield 36.0 + lag
        z_up2.wait_recv()
        z_down2.wait_recv()
        send_x(2)
        merge(0, 2)
        direct = h == 1 and s == 1 and not far_over_z
        if direct:
            last[2] = [spread(0, 2, 0, 64, x_far)]
        if not far_over_z:
            finish(0)
        yield 36.1 + lag
        pass_on(3)
        yield 36.2 + lag
        pass_on(1)
        if far_over_z:
            yield 37.0 + lag
            z_up3.wait_recv()
            last[2] = [spread(2, 3, 0, 32, zh_next)]
            z_down3.wait_recv()
            last[2].append(spread(2, 1, 32, 32, zh_prev))
            merge(2, 3)
            merge(2, 1)
        yield 39.5 + lag
        if direct:
            x_up[2].wait_recv()
            merge(3, 2)
            x_down[2].wait_recv()
            merge(1, 2)
        else:
            pass_on(2)
        if not far_over_z:
            finish(3)
            finish(1)
        yield 41.5 + lag
        finish(2)

    def join(x_at, zh_at, s):
        low = lane_low((64, 128))
        rows = ds((((x + x_at) % 4) * 4 + (zh + zh_at) % 4) * 128 + s * 64, 64, 64)
        first, second = outp[0, rows, :], outp[1, rows, :]
        out[rows, pl.ds(0, 128)] = jnp.where(low, first, swap_lanes(second))
        out[rows, pl.ds(128, 128)] = jnp.where(low, swap_lanes(first), second)

    def join_res(half):
        def join_rows(i, carry):
            low = lane_low((128, 128))
            rows = ds(i * 128, 128, 128)
            first, second = resp[0, half, rows, :], resp[1, half, rows, :]
            at = (k if half == 0 else 1 - k) * 2048 + i * 128
            res[ds(at, 128, 128), :] = jnp.where(low, first, swap_lanes(second))
            res[ds(at + 1024, 128, 128), :] = jnp.where(low, swap_lanes(first), second)
            return carry

        lax.fori_loop(0, 8, join_rows, 0)

    def side():
        yield 7.0
        load_nbr.wait()
        for copy in early["halo"]:
            copy.wait_recv()
        first = col * 2048 + row * 128 - HALO
        place = lax.broadcasted_iota(jnp.int32, (256, 128), 0) + first
        links = jnp.zeros((256, 128), F32)
        for index in range(8):
            links += (nbrv[pl.ds(index, 1), :] == place).astype(F32)
        links = links.astype(BF16)
        window = ext[ds(row * 128, 256, 128), :]
        high = window.astype(BF16)
        rest = (window - high.astype(F32)).astype(BF16)
        dims = (((0,), (0,)), ((), ()))
        near = lax.dot_general(links, high, dims, preferred_element_type=F32)
        near += lax.dot_general(links, rest, dims, preferred_element_type=F32)
        own = ext[ds(row * 128 + HALO, 128, 64), :]
        wide = own - 0.025 * (8.0 * own - near)
        left, right = wide[:, :128], wide[:, 128:]
        low = lane_low((128, 128))
        base[0] = jnp.where(low, left, swap_lanes(right))
        base[1] = jnp.where(low, swap_lanes(left), right)
        for shard in range(4):
            for s in range(2):
                rows = ds((x * 4 + shard) * 128 + s * 64, 64, 64)
                grcat[pl.ds(s * 256 + shard * 64, 64), pl.ds(0, 256)] = grv[rows, :]
        yield 16.4
        for d in range(1, 4):
            early["gr"][d - 1].wait_recv()
            for shard in range(4):
                for s in range(2):
                    rows = pl.ds(shard * 128 + s * 64, 64)
                    grcat[pl.ds(s * 256 + shard * 64, 64), pl.ds(d * 256, 256)] = grrecv[d - 1, rows, :].astype(BF16)
        yield 24.8
        join_res(0)
        yield 30.0
        for h in range(2):
            early[h].wait_recv()
        join_res(1)

    tasks = [(-10.0, 99, start())]
    while tasks:
        tasks.sort(key=lambda task: task[:2])
        _, number, task = tasks.pop(0)
        at = next(task, None)
        if at is not None:
            tasks.append((at, number, task))
        elif number == 99:
            tasks = [(0.0, 4, side()), (0.0, 5, prepare())]
            for h in range(2):
                tasks.append((0.0, 20 + h, backward(h)))
                for s in range(2):
                    tasks.append((0.0, 2 * h + s, forward(h, s)))
                    tasks.append((0.0, 10 + 2 * h + s, update(h, s)))
    for copy in sends:
        copy.wait_send()


def store(out_in, res_in, out, res, sem):
    copies = [
        pltpu.make_async_copy(out_in, out, sem.at[0]),
        pltpu.make_async_copy(res_in, res, sem.at[1]),
    ]
    for copy in copies:
        copy.start()
    for copy in copies:
        copy.wait()


def body(observed, slip, green_left, green_right, block_ranks, neighbours):
    vmem, dma = pltpu.VMEM, pltpu.SemaphoreType.DMA
    hbm = pl.BlockSpec(memory_space=pltpu.HBM)
    whole = pl.BlockSpec(memory_space=pltpu.VMEM)
    shapes = (
        jax.ShapeDtypeStruct((2048, 256), F32),
        jax.ShapeDtypeStruct((4096, 128), F32),
    )
    joined = pl.pallas_call(
        kernel,
        name="step",
        out_shape=tuple(vmem(shape.shape, F32) for shape in shapes),
        in_specs=[hbm, hbm, hbm, hbm, pl.BlockSpec(memory_space=pltpu.SMEM), hbm],
        out_specs=(whole, whole),
        scratch_shapes=[
            vmem((2048 + 2 * HALO, 256), F32),
            vmem((4096, 128), BF16),
            vmem((2048, 256), BF16),
            vmem((2, 2, 64, 128), F32),
            vmem((8, 128), jnp.int32),
            vmem((2048, 128), F32),
            vmem((2048, 128), F32),
            vmem((1024, 512), BF16),
            vmem((2048, 256), F32),
            vmem((3, 512, 256), F32),
            vmem((512, 1024), BF16),
            vmem((2, 256, 128), BF16),
            vmem((2, 2, 512, 128), F32),
            vmem((2, 2, 512, 128), F32),
            vmem((2, 2, 512, 128), F32),
            vmem((2, 2, 2, 64, 128), F32),
            vmem((2, 2, 64, 128), F32),
            vmem((2, 2, 2, 64, 128), F32),
            vmem((2, 2, 3, 64, 128), F32),
            vmem((2, 2, 64, 128), F32),
            vmem((2, 2, 1024, 128), F32),
            vmem((2, 64, 128), F32),
            vmem((2, 64, 128), F32),
            vmem((2, 4, 64, 128), F32),
            vmem((2, 1024, 128), BF16),
            vmem((2, 2, 256, 128), F32),
            vmem((2, 2, 2, 32, 128), F32),
            vmem((2, 2, 2, 2, 32, 128), F32),
            vmem((2, 2, 2, 32, 128), F32),
            vmem((2, 128, 128), F32),
            vmem((2, 2048, 128), F32),
            dma((N_SEM,)),
            dma((N_SEM,)),
            dma((32,)),
        ],
        compiler_params=pltpu.CompilerParams(
            collective_id=0, has_side_effects=True, vmem_limit_bytes=40 * 2**20
        ),
        cost_estimate=pl.CostEstimate(flops=10**9, bytes_accessed=12 * 2**20, transcendentals=0),
    )(*(pltpu.with_memory_space_constraint(value, pltpu.HBM) for value in (observed, slip, green_left, green_right)), block_ranks, pltpu.with_memory_space_constraint(neighbours.T, pltpu.HBM))
    return pl.pallas_call(
        store,
        name="store",
        out_shape=shapes,
        in_specs=[whole, whole],
        out_specs=(hbm, hbm),
        scratch_shapes=[dma((2,))],
        compiler_params=pltpu.CompilerParams(vmem_limit_bytes=4 * 2**20),
    )(*(pltpu.with_memory_space_constraint(value, pltpu.VMEM) for value in joined))


def solution(mesh):
    return jax.shard_map(
        body,
        mesh=mesh,
        in_specs=(
            P("row", None),
            P("col", None),
            P("row", "col"),
            P("col", "row"),
            P("row", "col"),
            P("col", None),
        ),
        out_specs=(P("col", None), P("row", None)),
        check_vma=False,
    )
```

```python
import jax
import jax.numpy as jnp
from jax import lax
from jax.experimental import pallas as pl
from jax.experimental.pallas import tpu as pltpu
from jax.sharding import PartitionSpec as P

MESH = pl.DeviceIdType.MESH
F32 = jnp.float32
BF16 = jnp.bfloat16
HALO = 64
N_SEM = 240
SUM_Z_FIRST, GATHER_Z_LAST = (), (1,)
LAG_FORWARD, LAG_BACK = 3.5, 4.2
FAR_OVER_Z = ((1, 0), (1, 1))


def lane_low(shape):
    return lax.broadcasted_iota(jnp.int32, shape, 1) < 64


def swap_lanes(value):
    return pltpu.roll(value, 64, 1)


def ds(start, size, unit):
    if isinstance(start, int):
        return pl.ds(start, size)
    return pl.ds(pl.multiple_of(start, unit), size)


def kernel(
    obs, slip, gl, gr, rank, nbr, out, res,
    ext, glv, grv, obsv, nbrv, glsend, glrecv, xy, grsend, grrecv, grcat,
    rhs, pred, psend, precv, azr, azs, ay, af, afs, resp, bsend, brecv, bx, bd, grad,
    cm1, cr, cm3, base, outp, send_sem, recv_sem, local_sem,
):
    row = lax.axis_index("row")
    col = lax.axis_index("col")
    x, zh = row // 4, row % 4
    zl, y, k = col // 8, (col // 2) % 4, col % 2

    def device(x, zh, zl, y, k):
        return (x * 4 + zh, (zl * 4 + y) * 2 + k)

    sibling = device(x, zh, zl, y, 1 - k)
    y_next = device(x, zh, zl, (y + 1) % 4, k)
    y_prev = device(x, zh, zl, (y + 3) % 4, k)
    y_far = device(x, zh, zl, (y + 2) % 4, k)
    z_pair = device(x, zh, 1 - zl, y, k)
    x_next = device((x + 1) % 4, zh, zl, y, k)
    x_prev = device((x + 3) % 4, zh, zl, y, k)
    x_far = device((x + 2) % 4, zh, zl, y, k)
    zh_next = device(x, (zh + 1) % 4, zl, y, k)
    zh_prev = device(x, (zh + 3) % 4, zl, y, k)
    col_next = (row, (col + 1) % 16)
    col_prev = (row, (col + 15) % 16)

    counts = [0, 0]
    sends = []

    def send(src, dst, to):
        index = counts[0]
        counts[0] += 1
        copy = pltpu.make_async_remote_copy(
            src_ref=src, dst_ref=dst, send_sem=send_sem.at[index], recv_sem=recv_sem.at[index],
            device_id=to, device_id_type=MESH,
        )
        copy.start()
        sends.append(copy)
        return copy

    def local(src, dst):
        index = counts[1]
        counts[1] += 1
        copy = pltpu.make_async_copy(src, dst, local_sem.at[index])
        copy.start()
        return copy

    partners = (
        sibling, col_next, col_prev, zh_next, zh_prev, x_next, x_prev, x_far, y_next, y_prev, y_far, z_pair,
    )

    load_gr, load_slip = [], []
    for piece in range(4):
        rows = pl.ds(piece * 512, 512)
        load_gr.append(local(gr.at[rows], grv.at[rows]))
        load_slip.append(local(slip.at[rows], ext.at[pl.ds(HALO + piece * 512, 512)]))
    load_gl = [
        local(gl.at[ds((1 - k) * 2048, 2048, 2048)], glv.at[pl.ds(2048, 2048)]),
        local(gl.at[ds(k * 2048, 2048, 2048)], glv.at[pl.ds(0, 2048)]),
    ]
    shard = y * 128 + zl * 64
    load_obs = [
        local(obs.at[ds(k * 2048 + half * 1024 + piece * 512 + shard, 64, 64)], obsv.at[half, piece])
        for half in range(2)
        for piece in range(2)
    ]
    load_nbr = local(nbr.at[:, ds(row * 128, 128, 128)], nbrv)

    barrier = pltpu.get_barrier_semaphore()
    for partner in partners:
        pl.semaphore_signal(barrier, inc=1, device_id=partner, device_id_type=MESH)

    keep = lax.broadcasted_iota(jnp.int32, (128, 128), 0) < rank[0, 0]
    keep_lane = lax.broadcasted_iota(jnp.int32, (256, 128), 1) < rank[0, 0]
    early = {}

    def share_right(s, first, size):
        def rows(at):
            return ds(((x + at) % 4) * 256 + first, size, 64)

        return [
            send(grsend.at[s, rows(at)], grrecv.at[slot, s, pl.ds(first, size)], to)
            for slot, at, to in ((1, 2, x_far), (0, 3, x_prev), (2, 1, x_next))
        ]

    def product(half, h, s):
        first = half * 2048 + s * 512
        pair = jnp.concatenate([glv[pl.ds(first, 512), :], glv[pl.ds(first + 1024, 512), :]], axis=1)
        return jnp.dot(pair, rhs[h], preferred_element_type=F32)

    def start():
        inner = jnp.zeros((128, 128), F32)
        for piece in range(4):
            load_gr[piece].wait()
            load_slip[piece].wait()
            for rake in range(2):
                lanes = pl.ds(rake * 128, 128)
                inner += lax.dot_general(
                    grv[pl.ds(piece * 512, 512), lanes],
                    ext[pl.ds(HALO + piece * 512, 512), lanes].astype(BF16),
                    (((0,), (0,)), ((), ())),
                    preferred_element_type=F32,
                )
        inner = jnp.where(keep, inner, 0.0).astype(BF16).astype(F32)
        low = lane_low((128, 128))
        turned = swap_lanes(inner)
        rhs[0, pl.ds(0, 128), :] = jnp.where(low, inner, 0.0).astype(BF16)
        rhs[0, pl.ds(128, 128), :] = jnp.where(low, 0.0, turned).astype(BF16)
        rhs[1, pl.ds(0, 128), :] = jnp.where(low, turned, 0.0).astype(BF16)
        rhs[1, pl.ds(128, 128), :] = jnp.where(low, 0.0, inner).astype(BF16)
        load_gl[0].wait()
        for h in range(2):
            for s in range(2):
                psend[h, s] = product(1, h, s)
        def widen_right(i, carry):
            for piece in range(2):
                rows = ds(i * 128 + piece * 64, 64, 64)
                grsend[piece, ds(i * 64, 64, 64), :] = grv[rows, :].astype(F32)
            return carry

        lax.fori_loop(0, 16, widen_right, 0)
        yield -9.0
        pl.semaphore_wait(barrier, len(partners))
        for h in range(2):
            for s in range(2):
                early["pred", h, s] = [
                    send(psend.at[h, s, pl.ds(i * 128, 128)], precv.at[h, s, pl.ds(i * 128, 128)], sibling)
                    for i in range(4)
                ]
        early["gr", 0] = share_right(0, 0, 256)
        early["gr", 1] = share_right(1, 0, 256)
        yield -8.0
        load_gl[1].wait()
        for h in range(2):
            for s in range(2):
                pred[h, s] = product(0, h, s)
        yield -7.0
        for copy in load_obs:
            copy.wait()

    def prepare():
        yield 1.0

        def widen_left(i, carry):
            rows = ds(i * 256, 256, 256)
            left = glv[ds(2048 + i * 256, 256, 256), :].astype(F32)
            glsend[rows, :] = jnp.where(keep_lane, left, 0.0)
            return carry

        lax.fori_loop(0, 8, widen_left, 0)
        early["gl"] = [
            send(glsend.at[pl.ds(i * 512, 512)], glrecv.at[pl.ds(i * 512, 512)], sibling) for i in range(4)
        ]
        early["halo"] = [
            send(ext.at[pl.ds(2048, HALO)], ext.at[pl.ds(0, HALO)], col_next),
            send(ext.at[pl.ds(HALO, HALO)], ext.at[pl.ds(2048 + HALO, HALO)], col_prev),
        ]
        yield 4.5

        def own_left(i, carry):
            rows = ds(i * 256, 256, 256)
            for half in range(2):
                left = glv[ds(half * 1024 + i * 256, 256, 256), :].astype(F32)
                xy[rows, pl.ds(half * 256, 128)] = jnp.where(keep_lane, left, 0.0).astype(BF16)
            return carry

        lax.fori_loop(0, 4, own_left, 0)
        yield 9.0
        for copy in early["gl"]:
            copy.wait_recv()

        def other_left(i, carry):
            rows = ds(i * 256, 256, 256)
            for half in range(2):
                xy[rows, pl.ds(half * 256 + 128, 128)] = glrecv[ds(half * 1024 + i * 256, 256, 256), :].astype(BF16)
            return carry

        lax.fori_loop(0, 4, other_left, 0)

    def forward(h, s):
        lag = LAG_FORWARD * h + 0.8 * s
        if h == 1:
            yield 2.0 + 0.1 * s
        values = pred.at[h, s]
        for copy in early["pred", h, s]:
            copy.wait_recv()
        values[...] += precv[h, s]

        def part(at, sub):
            return ds(((y + at) % 4) * 128 + sub * 64, 64, 64)

        other = 1 - zl
        z_first = h in SUM_Z_FIRST
        if z_first:
            pairs = [send(values.at[part(at, other)], azr.at[h, s, at], z_pair) for at in (2, 1, 3, 0)]
            yield 3.6 + lag
            for copy in pairs:
                copy.wait_recv()
            for slot, at in enumerate((1, 3, 2)):
                afs[h, s, slot] = values[part(at, zl), :] + azr[h, s, at]
            far = send(afs.at[h, s, 2], af.at[h, s, 2], y_far)
            up2 = send(afs.at[h, s, 0], af.at[h, s, 0], y_next)
            down2 = send(afs.at[h, s, 1], af.at[h, s, 1], y_prev)
            arrive = (far, up2, down2)
        else:
            pair1 = send(values.at[part(2, other)], azr.at[h, s, 1], z_pair)
            up1 = send(values.at[part(1, other)], ay.at[h, s, 0], y_next)
            down1 = send(values.at[part(3, other)], ay.at[h, s, 1], y_prev)
            up2 = send(values.at[part(1, zl)], af.at[h, s, 0], y_next)
            down2 = send(values.at[part(3, zl)], af.at[h, s, 1], y_prev)
            yield 3.0 + lag
            up1.wait_recv()
            down1.wait_recv()
            azs[h, s] = values[part(0, other), :] + ay[h, s, 0] + ay[h, s, 1]
            pair2 = send(azs.at[h, s], azr.at[h, s, 0], z_pair)
            pair1.wait_recv()
            afs[h, s, 2] = values[part(2, zl), :] + azr[h, s, 1]
            far = send(afs.at[h, s, 2], af.at[h, s, 2], y_far)
            arrive = (up2, down2, pair2, far)
        top, bottom = obsv[0, s], obsv[1, s]
        low = lane_low((64, 128))
        if h == 0:
            seen = jnp.where(low, top, swap_lanes(bottom))
        else:
            seen = jnp.where(low, swap_lanes(top), bottom)
        residual = resp.at[h, 0, pl.ds(s * 512, 512)]
        mine = residual.at[part(0, zl)]
        mine[...] = values[part(0, zl), :] - seen
        yield 6.8 + lag
        for copy in arrive:
            copy.wait_recv()
        mine[...] = mine[...] + af[h, s, 0] + af[h, s, 1] + af[h, s, 2] + azr[h, s, 0]

        def share(at, sub, to):
            shard = residual.at[part(at, sub)]
            return send(shard, shard, to)

        pair1 = share(0, zl, z_pair)
        far = share(0, zl, y_far)
        up1 = share(0, zl, y_next)
        down1 = share(0, zl, y_prev)
        yield 9.9 + lag
        if h in GATHER_Z_LAST:
            yield 10.4 + lag
            far.wait_recv()
            rest = [pair1, share(2, zl, z_pair)]
            up1.wait_recv()
            rest.append(share(3, zl, z_pair))
            down1.wait_recv()
            rest.append(share(1, zl, z_pair))
        else:
            pair1.wait_recv()
            rest = [up1, down1, share(0, other, y_next), share(0, other, y_prev)]
            yield 10.4 + lag
            far.wait_recv()
            rest.append(share(2, zl, z_pair))
        yield 13.6 + lag
        for copy in rest:
            copy.wait_recv()

    def backward(h):
        lag = LAG_BACK * h
        yield 14.5 + lag
        residual = resp.at[h, 0]
        low = lane_low((64, 128))
        acc = lax.dot_general(
            xy[...], residual[...].astype(BF16), (((0,), (0,)), ((), ())), preferred_element_type=F32
        )
        total = acc[:256] + swap_lanes(acc[256:])
        turned = swap_lanes(total)
        bsend[h] = jnp.where(low, total[128:192], turned[192:256])
        swap = send(bsend.at[h], brecv.at[h], sibling)
        mine = jnp.where(low, total[0:64], turned[64:128])
        yield 16.2 + lag
        swap.wait_recv()
        bx[h, 0] = (mine + brecv[h]).astype(BF16).astype(F32)
        shares = [
            send(bx.at[h, 0], bx.at[h, 2], x_far),
            send(bx.at[h, 0], bx.at[h, 1], x_prev),
            send(bx.at[h, 0], bx.at[h, 3], x_next),
        ]
        early[h] = send(residual, resp.at[h, 1], sibling)
        yield 19.6 + lag
        for copy in shares:
            copy.wait_recv()
        for d in range(4):
            packed = bx[h, d]
            turned = swap_lanes(packed)
            bd[h, pl.ds(d * 256, 64), :] = jnp.where(low, packed, 0.0).astype(BF16)
            bd[h, pl.ds(d * 256 + 64, 64), :] = jnp.where(low, turned, 0.0).astype(BF16)
            bd[h, pl.ds(d * 256 + 128, 64), :] = jnp.where(low, 0.0, turned).astype(BF16)
            bd[h, pl.ds(d * 256 + 192, 64), :] = jnp.where(low, 0.0, packed).astype(BF16)

    def update(h, s):
        lag = LAG_BACK * h + 0.8 * s
        yield 19.7 + LAG_BACK * h + (0.2, 0.01)[h] * s
        part_grad = grad.at[h, s]
        part_grad[...] = jnp.dot(grcat[pl.ds(s * 256, 256), :], bd[h], preferred_element_type=F32)

        def piece(at, sub):
            return ds(((zh + at) % 4) * 64 + sub * 32, 32, 32)

        up1 = send(part_grad.at[piece(2, 0)], cm1.at[h, s, 0], zh_next)
        down1 = send(part_grad.at[piece(2, 1)], cm1.at[h, s, 1], zh_prev)
        up2 = send(part_grad.at[piece(1, 1)], cr.at[h, s, 1, 0], zh_next)
        down2 = send(part_grad.at[piece(3, 0)], cr.at[h, s, 0, 1], zh_prev)
        yield 23.8 + lag
        up1.wait_recv()
        cm3[h, s, 0] = part_grad[piece(1, 0), :] + cm1[h, s, 0]
        up3 = send(cm3.at[h, s, 0], cr.at[h, s, 0, 0], zh_next)
        down1.wait_recv()
        cm3[h, s, 1] = part_grad[piece(3, 1), :] + cm1[h, s, 1]
        down3 = send(cm3.at[h, s, 1], cr.at[h, s, 1, 1], zh_prev)
        yield 27.6 + lag
        for copy in (up2, down2, up3, down3):
            copy.wait_recv()
        final = outp.at[h]
        for sub in range(2):
            total = part_grad[piece(0, sub), :] + cr[h, s, sub, 0] + cr[h, s, sub, 1]
            rows = ds(row * 128 + s * 64 + sub * 32, 32, 32)
            final[rows, :] = jnp.maximum(base[h, pl.ds(s * 64 + sub * 32, 32), :] - 0.5 * total, 0.0)

        def spread(x_at, zh_at, first, size, to):
            start = (((x + x_at) % 4) * 4 + (zh + zh_at) % 4) * 128 + s * 64 + first
            rows = ds(start, size, 32)
            return send(final.at[rows], final.at[rows], to)

        def merge(x_at, zh_at):
            if h == 1:
                join(x_at, zh_at, s)

        far_over_z = (h, s) in FAR_OVER_Z
        z_up1 = spread(0, 0, 0, 64, zh_next)
        z_down1 = spread(0, 0, 0, 64, zh_prev)
        x_up, x_down, last = {}, {}, {}
        x_up[0] = spread(0, 0, 0, 64, x_next)
        x_down[0] = spread(0, 0, 0, 64, x_prev)
        if far_over_z:
            far = spread(0, 0, 0, 64, x_far)

        def send_x(at):
            x_up[at] = spread(0, at, 0, 64, x_next)
            x_down[at] = spread(0, at, 0, 64, x_prev)

        def pass_on(at):
            x_up[at].wait_recv()
            if not far_over_z:
                last[at] = [spread(3, at, 0, 32, x_next)]
            x_down[at].wait_recv()
            if not far_over_z:
                last[at].append(spread(1, at, 32, 32, x_prev))
            merge(3, at)
            merge(1, at)

        def finish(at):
            for copy in last[at]:
                copy.wait_recv()
            merge(2, at)

        yield 30.7 + lag
        merge(0, 0)
        pass_on(0)
        yield 32.2 + lag
        z_up1.wait_recv()
        z_up2 = spread(0, 3, 0, 32, zh_next)
        send_x(3)
        z_down1.wait_recv()
        z_down2 = spread(0, 1, 32, 32, zh_prev)
        send_x(1)
        merge(0, 3)
        merge(0, 1)
        if far_over_z:
            yield 32.3 + lag
            far.wait_recv()
            z_up3 = spread(2, 0, 0, 64, zh_next)
            z_down3 = spread(2, 0, 0, 64, zh_prev)
            merge(2, 0)
        yield 36.0 + lag
        z_up2.wait_recv()
        z_down2.wait_recv()
        send_x(2)
        merge(0, 2)
        direct = h == 1 and s == 1 and not far_over_z
        if direct:
            last[2] = [spread(0, 2, 0, 64, x_far)]
        if not far_over_z:
            finish(0)
        yield 36.1 + lag
        pass_on(3)
        yield 36.2 + lag
        pass_on(1)
        if far_over_z:
            yield 37.0 + lag
            z_up3.wait_recv()
            last[2] = [spread(2, 3, 0, 32, zh_next)]
            z_down3.wait_recv()
            last[2].append(spread(2, 1, 32, 32, zh_prev))
            merge(2, 3)
            merge(2, 1)
        yield 39.5 + lag
        if direct:
            x_up[2].wait_recv()
            merge(3, 2)
            x_down[2].wait_recv()
            merge(1, 2)
        else:
            pass_on(2)
        if not far_over_z:
            finish(3)
            finish(1)
        yield 41.5 + lag
        finish(2)

    def join(x_at, zh_at, s):
        low = lane_low((64, 128))
        rows = ds((((x + x_at) % 4) * 4 + (zh + zh_at) % 4) * 128 + s * 64, 64, 64)
        first, second = outp[0, rows, :], outp[1, rows, :]
        out[rows, pl.ds(0, 128)] = jnp.where(low, first, swap_lanes(second))
        out[rows, pl.ds(128, 128)] = jnp.where(low, swap_lanes(first), second)

    def join_res(half):
        def join_rows(i, carry):
            low = lane_low((128, 128))
            rows = ds(i * 128, 128, 128)
            first, second = resp[0, half, rows, :], resp[1, half, rows, :]
            at = (k if half == 0 else 1 - k) * 2048 + i * 128
            res[ds(at, 128, 128), :] = jnp.where(low, first, swap_lanes(second))
            res[ds(at + 1024, 128, 128), :] = jnp.where(low, swap_lanes(first), second)
            return carry

        lax.fori_loop(0, 8, join_rows, 0)

    def side():
        yield 7.0
        load_nbr.wait()
        for copy in early["halo"]:
            copy.wait_recv()
        first = col * 2048 + row * 128 - HALO
        place = lax.broadcasted_iota(jnp.int32, (256, 128), 0) + first
        links = jnp.zeros((256, 128), F32)
        for index in range(8):
            links += (nbrv[pl.ds(index, 1), :] == place).astype(F32)
        links = links.astype(BF16)
        window = ext[ds(row * 128, 256, 128), :]
        high = window.astype(BF16)
        rest = (window - high.astype(F32)).astype(BF16)
        dims = (((0,), (0,)), ((), ()))
        near = lax.dot_general(links, high, dims, preferred_element_type=F32)
        near += lax.dot_general(links, rest, dims, preferred_element_type=F32)
        own = ext[ds(row * 128 + HALO, 128, 64), :]
        wide = own - 0.025 * (8.0 * own - near)
        left, right = wide[:, :128], wide[:, 128:]
        low = lane_low((128, 128))
        base[0] = jnp.where(low, left, swap_lanes(right))
        base[1] = jnp.where(low, swap_lanes(left), right)
        for shard in range(4):
            for s in range(2):
                rows = ds((x * 4 + shard) * 128 + s * 64, 64, 64)
                grcat[pl.ds(s * 256 + shard * 64, 64), pl.ds(0, 256)] = grv[rows, :]
        for s in range(2):
            yield (13.7, 19.8)[s]
            for copy in early["gr", s]:
                copy.wait_recv()
            for d in range(1, 4):
                grcat[pl.ds(s * 256, 256), pl.ds(d * 256, 256)] = grrecv[d - 1, s].astype(BF16)
        yield 24.8
        join_res(0)
        yield 30.0
        for h in range(2):
            early[h].wait_recv()
        join_res(1)

    tasks = [(-10.0, 99, start())]
    while tasks:
        tasks.sort(key=lambda task: task[:2])
        _, number, task = tasks.pop(0)
        at = next(task, None)
        if at is not None:
            tasks.append((at, number, task))
        elif number == 99:
            tasks = [(0.0, 4, side()), (0.0, 5, prepare())]
            for h in range(2):
                tasks.append((0.0, 20 + h, backward(h)))
                for s in range(2):
                    tasks.append((0.0, 2 * h + s, forward(h, s)))
                    tasks.append((0.0, 10 + 2 * h + s, update(h, s)))
    for copy in sends:
        copy.wait_send()


def store(out_in, res_in, out, res, sem):
    copies = [
        pltpu.make_async_copy(out_in, out, sem.at[0]),
        pltpu.make_async_copy(res_in, res, sem.at[1]),
    ]
    for copy in copies:
        copy.start()
    for copy in copies:
        copy.wait()


def body(observed, slip, green_left, green_right, block_ranks, neighbours):
    vmem, dma = pltpu.VMEM, pltpu.SemaphoreType.DMA
    hbm = pl.BlockSpec(memory_space=pltpu.HBM)
    whole = pl.BlockSpec(memory_space=pltpu.VMEM)
    shapes = (
        jax.ShapeDtypeStruct((2048, 256), F32),
        jax.ShapeDtypeStruct((4096, 128), F32),
    )
    joined = pl.pallas_call(
        kernel,
        name="step",
        out_shape=tuple(vmem(shape.shape, F32) for shape in shapes),
        in_specs=[hbm, hbm, hbm, hbm, pl.BlockSpec(memory_space=pltpu.SMEM), hbm],
        out_specs=(whole, whole),
        scratch_shapes=[
            vmem((2048 + 2 * HALO, 256), F32),
            vmem((4096, 128), BF16),
            vmem((2048, 256), BF16),
            vmem((2, 2, 64, 128), F32),
            vmem((8, 128), jnp.int32),
            vmem((2048, 128), F32),
            vmem((2048, 128), F32),
            vmem((1024, 512), BF16),
            vmem((2, 1024, 256), F32),
            vmem((3, 2, 256, 256), F32),
            vmem((512, 1024), BF16),
            vmem((2, 256, 128), BF16),
            vmem((2, 2, 512, 128), F32),
            vmem((2, 2, 512, 128), F32),
            vmem((2, 2, 512, 128), F32),
            vmem((2, 2, 4, 64, 128), F32),
            vmem((2, 2, 64, 128), F32),
            vmem((2, 2, 2, 64, 128), F32),
            vmem((2, 2, 3, 64, 128), F32),
            vmem((2, 2, 3, 64, 128), F32),
            vmem((2, 2, 1024, 128), F32),
            vmem((2, 64, 128), F32),
            vmem((2, 64, 128), F32),
            vmem((2, 4, 64, 128), F32),
            vmem((2, 1024, 128), BF16),
            vmem((2, 2, 256, 128), F32),
            vmem((2, 2, 2, 32, 128), F32),
            vmem((2, 2, 2, 2, 32, 128), F32),
            vmem((2, 2, 2, 32, 128), F32),
            vmem((2, 128, 128), F32),
            vmem((2, 2048, 128), F32),
            dma((N_SEM,)),
            dma((N_SEM,)),
            dma((32,)),
        ],
        compiler_params=pltpu.CompilerParams(
            collective_id=0, has_side_effects=True, vmem_limit_bytes=40 * 2**20
        ),
        cost_estimate=pl.CostEstimate(flops=10**9, bytes_accessed=12 * 2**20, transcendentals=0),
    )(*(pltpu.with_memory_space_constraint(value, pltpu.HBM) for value in (observed, slip, green_left, green_right)), block_ranks, pltpu.with_memory_space_constraint(neighbours.T, pltpu.HBM))
    return pl.pallas_call(
        store,
        name="store",
        out_shape=shapes,
        in_specs=[whole, whole],
        out_specs=(hbm, hbm),
        scratch_shapes=[dma((2,))],
        compiler_params=pltpu.CompilerParams(vmem_limit_bytes=4 * 2**20),
    )(*(pltpu.with_memory_space_constraint(value, pltpu.VMEM) for value in joined))


def solution(mesh):
    return jax.shard_map(
        body,
        mesh=mesh,
        in_specs=(
            P("row", None),
            P("col", None),
            P("row", "col"),
            P("col", "row"),
            P("row", "col"),
            P("col", None),
        ),
        out_specs=(P("col", None), P("row", None)),
        check_vma=False,
    )
```

```python
import jax
import jax.numpy as jnp
from jax import lax
from jax.experimental import pallas as pl
from jax.experimental.pallas import tpu as pltpu
from jax.sharding import PartitionSpec as P

MESH = pl.DeviceIdType.MESH
F32 = jnp.float32
BF16 = jnp.bfloat16
HALO = 64
N_SEM = 240
SUM_Z_FIRST, GATHER_Z_LAST = (), (1,)
LAG_FORWARD, LAG_BACK = 3.5, 4.2
FAR_OVER_Z = ((1, 0), (1, 1))


def lane_low(shape):
    return lax.broadcasted_iota(jnp.int32, shape, 1) < 64


def swap_lanes(value):
    return pltpu.roll(value, 64, 1)


def ds(start, size, unit):
    if isinstance(start, int):
        return pl.ds(start, size)
    return pl.ds(pl.multiple_of(start, unit), size)


def kernel(
    obs, slip, gl, gr, rank, nbr, out, res,
    ext, glv, grv, obsv, nbrv, glsend, glrecv, xy, grsend, grrecv, grcat,
    rhs, pred, psend, precv, azr, azs, ay, af, afs, resp, bsend, brecv, bx, bd, grad,
    cm1, cr, cm3, base, outp, send_sem, recv_sem, local_sem,
):
    row = lax.axis_index("row")
    col = lax.axis_index("col")
    x, zh = row // 4, row % 4
    zl, y, k = col // 8, (col // 2) % 4, col % 2

    def device(x, zh, zl, y, k):
        return (x * 4 + zh, (zl * 4 + y) * 2 + k)

    sibling = device(x, zh, zl, y, 1 - k)
    y_next = device(x, zh, zl, (y + 1) % 4, k)
    y_prev = device(x, zh, zl, (y + 3) % 4, k)
    y_far = device(x, zh, zl, (y + 2) % 4, k)
    z_pair = device(x, zh, 1 - zl, y, k)
    x_next = device((x + 1) % 4, zh, zl, y, k)
    x_prev = device((x + 3) % 4, zh, zl, y, k)
    x_far = device((x + 2) % 4, zh, zl, y, k)
    zh_next = device(x, (zh + 1) % 4, zl, y, k)
    zh_prev = device(x, (zh + 3) % 4, zl, y, k)
    col_next = (row, (col + 1) % 16)
    col_prev = (row, (col + 15) % 16)

    counts = [0, 0]
    sends = []

    def send(src, dst, to):
        index = counts[0]
        counts[0] += 1
        copy = pltpu.make_async_remote_copy(
            src_ref=src, dst_ref=dst, send_sem=send_sem.at[index], recv_sem=recv_sem.at[index],
            device_id=to, device_id_type=MESH,
        )
        copy.start()
        sends.append(copy)
        return copy

    def local(src, dst):
        index = counts[1]
        counts[1] += 1
        copy = pltpu.make_async_copy(src, dst, local_sem.at[index])
        copy.start()
        return copy

    partners = (
        sibling, col_next, col_prev, zh_next, zh_prev, x_next, x_prev, x_far, y_next, y_prev, y_far, z_pair,
    )

    load_gr, load_slip = [], []
    for piece in range(4):
        rows = pl.ds(piece * 512, 512)
        load_gr.append(local(gr.at[rows], grv.at[rows]))
        load_slip.append(local(slip.at[rows], ext.at[pl.ds(HALO + piece * 512, 512)]))
    load_gl = [
        local(gl.at[ds((1 - k) * 2048, 2048, 2048)], glv.at[pl.ds(2048, 2048)]),
        local(gl.at[ds(k * 2048, 2048, 2048)], glv.at[pl.ds(0, 2048)]),
    ]
    shard = y * 128 + zl * 64
    load_obs = [
        local(obs.at[ds(k * 2048 + half * 1024 + piece * 512 + shard, 64, 64)], obsv.at[half, piece])
        for half in range(2)
        for piece in range(2)
    ]
    load_nbr = local(nbr.at[:, ds(row * 128, 128, 128)], nbrv)

    barrier = pltpu.get_barrier_semaphore()
    for partner in partners:
        pl.semaphore_signal(barrier, inc=1, device_id=partner, device_id_type=MESH)

    keep = lax.broadcasted_iota(jnp.int32, (128, 128), 0) < rank[0, 0]
    keep_lane = lax.broadcasted_iota(jnp.int32, (256, 128), 1) < rank[0, 0]
    early = {}

    def share_right(s, first, size):
        def rows(at):
            return ds(((x + at) % 4) * 256 + first, size, 64)

        return [
            send(grsend.at[s, rows(at)], grrecv.at[slot, s, pl.ds(first, size)], to)
            for slot, at, to in ((1, 2, x_far), (0, 3, x_prev), (2, 1, x_next))
        ]

    def product(half, h, s):
        first = half * 2048 + s * 512
        pair = jnp.concatenate([glv[pl.ds(first, 512), :], glv[pl.ds(first + 1024, 512), :]], axis=1)
        return jnp.dot(pair, rhs[h], preferred_element_type=F32)

    def start():
        inner = jnp.zeros((128, 128), F32)
        for piece in range(4):
            load_gr[piece].wait()
            load_slip[piece].wait()
            for rake in range(2):
                lanes = pl.ds(rake * 128, 128)
                inner += lax.dot_general(
                    grv[pl.ds(piece * 512, 512), lanes],
                    ext[pl.ds(HALO + piece * 512, 512), lanes].astype(BF16),
                    (((0,), (0,)), ((), ())),
                    preferred_element_type=F32,
                )
        inner = jnp.where(keep, inner, 0.0).astype(BF16).astype(F32)
        low = lane_low((128, 128))
        turned = swap_lanes(inner)
        rhs[0, pl.ds(0, 128), :] = jnp.where(low, inner, 0.0).astype(BF16)
        rhs[0, pl.ds(128, 128), :] = jnp.where(low, 0.0, turned).astype(BF16)
        rhs[1, pl.ds(0, 128), :] = jnp.where(low, turned, 0.0).astype(BF16)
        rhs[1, pl.ds(128, 128), :] = jnp.where(low, 0.0, inner).astype(BF16)
        load_gl[0].wait()
        for s in range(2):
            psend[0, s] = product(1, 0, s)

        def swap_products(h):
            for s in range(2):
                early["pred", h, s] = [
                    send(psend.at[h, s, pl.ds(i * 128, 128)], precv.at[h, s, pl.ds(i * 128, 128)], sibling)
                    for i in range(4)
                ]

        yield -9.0
        pl.semaphore_wait(barrier, len(partners))
        swap_products(0)

        def widen_right(i, carry):
            for piece in range(2):
                rows = ds(i * 128 + piece * 64, 64, 64)
                grsend[piece, ds(i * 64, 64, 64), :] = grv[rows, :].astype(F32)
            return carry

        lax.fori_loop(0, 16, widen_right, 0)
        early["gr", 0] = share_right(0, 0, 256)
        early["gr", 1] = share_right(1, 0, 256)
        for s in range(2):
            psend[1, s] = product(1, 1, s)
        swap_products(1)
        yield -8.0
        load_gl[1].wait()
        for h in range(2):
            for s in range(2):
                pred[h, s] = product(0, h, s)
        yield -7.0
        for copy in load_obs:
            copy.wait()

    def prepare():
        yield 1.0

        def widen_left(i, carry):
            rows = ds(i * 256, 256, 256)
            left = glv[ds(2048 + i * 256, 256, 256), :].astype(F32)
            glsend[rows, :] = jnp.where(keep_lane, left, 0.0)
            return carry

        lax.fori_loop(0, 8, widen_left, 0)
        early["gl"] = [
            send(glsend.at[pl.ds(i * 512, 512)], glrecv.at[pl.ds(i * 512, 512)], sibling) for i in range(4)
        ]
        early["halo"] = [
            send(ext.at[pl.ds(2048, HALO)], ext.at[pl.ds(0, HALO)], col_next),
            send(ext.at[pl.ds(HALO, HALO)], ext.at[pl.ds(2048 + HALO, HALO)], col_prev),
        ]
        yield 4.5

        def own_left(i, carry):
            rows = ds(i * 256, 256, 256)
            for half in range(2):
                left = glv[ds(half * 1024 + i * 256, 256, 256), :].astype(F32)
                xy[rows, pl.ds(half * 256, 128)] = jnp.where(keep_lane, left, 0.0).astype(BF16)
            return carry

        lax.fori_loop(0, 4, own_left, 0)
        yield 9.0
        for copy in early["gl"]:
            copy.wait_recv()

        def other_left(i, carry):
            rows = ds(i * 256, 256, 256)
            for half in range(2):
                xy[rows, pl.ds(half * 256 + 128, 128)] = glrecv[ds(half * 1024 + i * 256, 256, 256), :].astype(BF16)
            return carry

        lax.fori_loop(0, 4, other_left, 0)

    def forward(h, s):
        lag = LAG_FORWARD * h + 0.8 * s
        if h == 1:
            yield 2.0 + 0.1 * s
        values = pred.at[h, s]
        for copy in early["pred", h, s]:
            copy.wait_recv()
        values[...] += precv[h, s]

        def part(at, sub):
            return ds(((y + at) % 4) * 128 + sub * 64, 64, 64)

        other = 1 - zl
        z_first = h in SUM_Z_FIRST
        if z_first:
            pairs = [send(values.at[part(at, other)], azr.at[h, s, at], z_pair) for at in (2, 1, 3, 0)]
            yield 3.6 + lag
            for copy in pairs:
                copy.wait_recv()
            for slot, at in enumerate((1, 3, 2)):
                afs[h, s, slot] = values[part(at, zl), :] + azr[h, s, at]
            far = send(afs.at[h, s, 2], af.at[h, s, 2], y_far)
            up2 = send(afs.at[h, s, 0], af.at[h, s, 0], y_next)
            down2 = send(afs.at[h, s, 1], af.at[h, s, 1], y_prev)
            arrive = (far, up2, down2)
        else:
            pair1 = send(values.at[part(2, other)], azr.at[h, s, 1], z_pair)
            up1 = send(values.at[part(1, other)], ay.at[h, s, 0], y_next)
            down1 = send(values.at[part(3, other)], ay.at[h, s, 1], y_prev)
            up2 = send(values.at[part(1, zl)], af.at[h, s, 0], y_next)
            down2 = send(values.at[part(3, zl)], af.at[h, s, 1], y_prev)
            yield 3.0 + lag
            up1.wait_recv()
            down1.wait_recv()
            azs[h, s] = values[part(0, other), :] + ay[h, s, 0] + ay[h, s, 1]
            pair2 = send(azs.at[h, s], azr.at[h, s, 0], z_pair)
            pair1.wait_recv()
            afs[h, s, 2] = values[part(2, zl), :] + azr[h, s, 1]
            far = send(afs.at[h, s, 2], af.at[h, s, 2], y_far)
            arrive = (up2, down2, pair2, far)
        top, bottom = obsv[0, s], obsv[1, s]
        low = lane_low((64, 128))
        if h == 0:
            seen = jnp.where(low, top, swap_lanes(bottom))
        else:
            seen = jnp.where(low, swap_lanes(top), bottom)
        residual = resp.at[h, 0, pl.ds(s * 512, 512)]
        mine = residual.at[part(0, zl)]
        mine[...] = values[part(0, zl), :] - seen
        yield 6.8 + lag
        for copy in arrive:
            copy.wait_recv()
        mine[...] = mine[...] + af[h, s, 0] + af[h, s, 1] + af[h, s, 2] + azr[h, s, 0]

        def share(at, sub, to):
            shard = residual.at[part(at, sub)]
            return send(shard, shard, to)

        pair1 = share(0, zl, z_pair)
        far = share(0, zl, y_far)
        up1 = share(0, zl, y_next)
        down1 = share(0, zl, y_prev)
        yield 9.9 + lag
        if h in GATHER_Z_LAST:
            yield 10.4 + lag
            far.wait_recv()
            rest = [pair1, share(2, zl, z_pair)]
            up1.wait_recv()
            rest.append(share(3, zl, z_pair))
            down1.wait_recv()
            rest.append(share(1, zl, z_pair))
        else:
            pair1.wait_recv()
            rest = [up1, down1, share(0, other, y_next), share(0, other, y_prev)]
            yield 10.4 + lag
            far.wait_recv()
            rest.append(share(2, zl, z_pair))
        yield 13.6 + lag
        for copy in rest:
            copy.wait_recv()

    def backward(h):
        lag = LAG_BACK * h
        yield 14.5 + lag
        residual = resp.at[h, 0]
        low = lane_low((64, 128))
        acc = lax.dot_general(
            xy[...], residual[...].astype(BF16), (((0,), (0,)), ((), ())), preferred_element_type=F32
        )
        total = acc[:256] + swap_lanes(acc[256:])
        turned = swap_lanes(total)
        bsend[h] = jnp.where(low, total[128:192], turned[192:256])
        swap = send(bsend.at[h], brecv.at[h], sibling)
        mine = jnp.where(low, total[0:64], turned[64:128])
        yield 16.2 + lag
        swap.wait_recv()
        bx[h, 0] = (mine + brecv[h]).astype(BF16).astype(F32)
        shares = [
            send(bx.at[h, 0], bx.at[h, 2], x_far),
            send(bx.at[h, 0], bx.at[h, 1], x_prev),
            send(bx.at[h, 0], bx.at[h, 3], x_next),
        ]
        early[h] = send(residual, resp.at[h, 1], sibling)
        yield 19.6 + lag
        for copy in shares:
            copy.wait_recv()
        for d in range(4):
            packed = bx[h, d]
            turned = swap_lanes(packed)
            bd[h, pl.ds(d * 256, 64), :] = jnp.where(low, packed, 0.0).astype(BF16)
            bd[h, pl.ds(d * 256 + 64, 64), :] = jnp.where(low, turned, 0.0).astype(BF16)
            bd[h, pl.ds(d * 256 + 128, 64), :] = jnp.where(low, 0.0, turned).astype(BF16)
            bd[h, pl.ds(d * 256 + 192, 64), :] = jnp.where(low, 0.0, packed).astype(BF16)

    def update(h, s):
        lag = LAG_BACK * h + 0.8 * s
        yield 19.7 + LAG_BACK * h + (0.2, 0.01)[h] * s
        part_grad = grad.at[h, s]
        part_grad[...] = jnp.dot(grcat[pl.ds(s * 256, 256), :], bd[h], preferred_element_type=F32)

        def piece(at, sub):
            return ds(((zh + at) % 4) * 64 + sub * 32, 32, 32)

        up1 = send(part_grad.at[piece(2, 0)], cm1.at[h, s, 0], zh_next)
        down1 = send(part_grad.at[piece(2, 1)], cm1.at[h, s, 1], zh_prev)
        up2 = send(part_grad.at[piece(1, 1)], cr.at[h, s, 1, 0], zh_next)
        down2 = send(part_grad.at[piece(3, 0)], cr.at[h, s, 0, 1], zh_prev)
        yield 23.8 + lag
        up1.wait_recv()
        cm3[h, s, 0] = part_grad[piece(1, 0), :] + cm1[h, s, 0]
        up3 = send(cm3.at[h, s, 0], cr.at[h, s, 0, 0], zh_next)
        down1.wait_recv()
        cm3[h, s, 1] = part_grad[piece(3, 1), :] + cm1[h, s, 1]
        down3 = send(cm3.at[h, s, 1], cr.at[h, s, 1, 1], zh_prev)
        yield 27.6 + lag
        for copy in (up2, down2, up3, down3):
            copy.wait_recv()
        final = outp.at[h]
        for sub in range(2):
            total = part_grad[piece(0, sub), :] + cr[h, s, sub, 0] + cr[h, s, sub, 1]
            rows = ds(row * 128 + s * 64 + sub * 32, 32, 32)
            final[rows, :] = jnp.maximum(base[h, pl.ds(s * 64 + sub * 32, 32), :] - 0.5 * total, 0.0)

        def spread(x_at, zh_at, first, size, to):
            start = (((x + x_at) % 4) * 4 + (zh + zh_at) % 4) * 128 + s * 64 + first
            rows = ds(start, size, 32)
            return send(final.at[rows], final.at[rows], to)

        def merge(x_at, zh_at):
            if h == 1:
                join(x_at, zh_at, s)

        far_over_z = (h, s) in FAR_OVER_Z
        z_up1 = spread(0, 0, 0, 64, zh_next)
        z_down1 = spread(0, 0, 0, 64, zh_prev)
        x_up, x_down, last = {}, {}, {}
        x_up[0] = spread(0, 0, 0, 64, x_next)
        x_down[0] = spread(0, 0, 0, 64, x_prev)
        if far_over_z:
            far = spread(0, 0, 0, 64, x_far)

        def send_x(at):
            x_up[at] = spread(0, at, 0, 64, x_next)
            x_down[at] = spread(0, at, 0, 64, x_prev)

        def pass_on(at):
            x_up[at].wait_recv()
            if not far_over_z:
                last[at] = [spread(3, at, 0, 32, x_next)]
            x_down[at].wait_recv()
            if not far_over_z:
                last[at].append(spread(1, at, 32, 32, x_prev))
            merge(3, at)
            merge(1, at)

        def finish(at):
            for copy in last[at]:
                copy.wait_recv()
            merge(2, at)

        yield 30.7 + lag
        merge(0, 0)
        pass_on(0)
        yield 32.2 + lag
        z_up1.wait_recv()
        z_up2 = spread(0, 3, 0, 32, zh_next)
        send_x(3)
        z_down1.wait_recv()
        z_down2 = spread(0, 1, 32, 32, zh_prev)
        send_x(1)
        merge(0, 3)
        merge(0, 1)
        if far_over_z:
            yield 32.3 + lag
            far.wait_recv()
            z_up3 = spread(2, 0, 0, 64, zh_next)
            z_down3 = spread(2, 0, 0, 64, zh_prev)
            merge(2, 0)
        yield 36.0 + lag
        z_up2.wait_recv()
        z_down2.wait_recv()
        send_x(2)
        merge(0, 2)
        direct = h == 1 and s == 1 and not far_over_z
        if direct:
            last[2] = [spread(0, 2, 0, 64, x_far)]
        if not far_over_z:
            finish(0)
        yield 36.1 + lag
        pass_on(3)
        yield 36.2 + lag
        pass_on(1)
        if far_over_z:
            yield 37.0 + lag
            z_up3.wait_recv()
            last[2] = [spread(2, 3, 0, 32, zh_next)]
            z_down3.wait_recv()
            last[2].append(spread(2, 1, 32, 32, zh_prev))
            merge(2, 3)
            merge(2, 1)
        yield 39.5 + lag
        if direct:
            x_up[2].wait_recv()
            merge(3, 2)
            x_down[2].wait_recv()
            merge(1, 2)
        else:
            pass_on(2)
        if not far_over_z:
            finish(3)
            finish(1)
        yield 41.5 + lag
        finish(2)

    def join(x_at, zh_at, s):
        low = lane_low((64, 128))
        rows = ds((((x + x_at) % 4) * 4 + (zh + zh_at) % 4) * 128 + s * 64, 64, 64)
        first, second = outp[0, rows, :], outp[1, rows, :]
        out[rows, pl.ds(0, 128)] = jnp.where(low, first, swap_lanes(second))
        out[rows, pl.ds(128, 128)] = jnp.where(low, swap_lanes(first), second)

    def join_res(half):
        def join_rows(i, carry):
            low = lane_low((128, 128))
            rows = ds(i * 128, 128, 128)
            first, second = resp[0, half, rows, :], resp[1, half, rows, :]
            at = (k if half == 0 else 1 - k) * 2048 + i * 128
            res[ds(at, 128, 128), :] = jnp.where(low, first, swap_lanes(second))
            res[ds(at + 1024, 128, 128), :] = jnp.where(low, swap_lanes(first), second)
            return carry

        lax.fori_loop(0, 8, join_rows, 0)

    def side():
        yield 7.0
        load_nbr.wait()
        for copy in early["halo"]:
            copy.wait_recv()
        first = col * 2048 + row * 128 - HALO
        place = lax.broadcasted_iota(jnp.int32, (256, 128), 0) + first
        links = jnp.zeros((256, 128), F32)
        for index in range(8):
            links += (nbrv[pl.ds(index, 1), :] == place).astype(F32)
        links = links.astype(BF16)
        window = ext[ds(row * 128, 256, 128), :]
        high = window.astype(BF16)
        rest = (window - high.astype(F32)).astype(BF16)
        dims = (((0,), (0,)), ((), ()))
        near = lax.dot_general(links, high, dims, preferred_element_type=F32)
        near += lax.dot_general(links, rest, dims, preferred_element_type=F32)
        own = ext[ds(row * 128 + HALO, 128, 64), :]
        wide = own - 0.025 * (8.0 * own - near)
        left, right = wide[:, :128], wide[:, 128:]
        low = lane_low((128, 128))
        base[0] = jnp.where(low, left, swap_lanes(right))
        base[1] = jnp.where(low, swap_lanes(left), right)
        for shard in range(4):
            for s in range(2):
                rows = ds((x * 4 + shard) * 128 + s * 64, 64, 64)
                grcat[pl.ds(s * 256 + shard * 64, 64), pl.ds(0, 256)] = grv[rows, :]
        for s in range(2):
            yield (13.7, 19.8)[s]
            for copy in early["gr", s]:
                copy.wait_recv()
            for d in range(1, 4):
                grcat[pl.ds(s * 256, 256), pl.ds(d * 256, 256)] = grrecv[d - 1, s].astype(BF16)
        yield 24.8
        join_res(0)
        yield 30.0
        for h in range(2):
            early[h].wait_recv()
        join_res(1)

    tasks = [(-10.0, 99, start())]
    while tasks:
        tasks.sort(key=lambda task: task[:2])
        _, number, task = tasks.pop(0)
        at = next(task, None)
        if at is not None:
            tasks.append((at, number, task))
        elif number == 99:
            tasks = [(0.0, 4, side()), (0.0, 5, prepare())]
            for h in range(2):
                tasks.append((0.0, 20 + h, backward(h)))
                for s in range(2):
                    tasks.append((0.0, 2 * h + s, forward(h, s)))
                    tasks.append((0.0, 10 + 2 * h + s, update(h, s)))
    for copy in sends:
        copy.wait_send()


def store(out_in, res_in, out, res, sem):
    copies = [
        pltpu.make_async_copy(out_in, out, sem.at[0]),
        pltpu.make_async_copy(res_in, res, sem.at[1]),
    ]
    for copy in copies:
        copy.start()
    for copy in copies:
        copy.wait()


def body(observed, slip, green_left, green_right, block_ranks, neighbours):
    vmem, dma = pltpu.VMEM, pltpu.SemaphoreType.DMA
    hbm = pl.BlockSpec(memory_space=pltpu.HBM)
    whole = pl.BlockSpec(memory_space=pltpu.VMEM)
    shapes = (
        jax.ShapeDtypeStruct((2048, 256), F32),
        jax.ShapeDtypeStruct((4096, 128), F32),
    )
    joined = pl.pallas_call(
        kernel,
        name="step",
        out_shape=tuple(vmem(shape.shape, F32) for shape in shapes),
        in_specs=[hbm, hbm, hbm, hbm, pl.BlockSpec(memory_space=pltpu.SMEM), hbm],
        out_specs=(whole, whole),
        scratch_shapes=[
            vmem((2048 + 2 * HALO, 256), F32),
            vmem((4096, 128), BF16),
            vmem((2048, 256), BF16),
            vmem((2, 2, 64, 128), F32),
            vmem((8, 128), jnp.int32),
            vmem((2048, 128), F32),
            vmem((2048, 128), F32),
            vmem((1024, 512), BF16),
            vmem((2, 1024, 256), F32),
            vmem((3, 2, 256, 256), F32),
            vmem((512, 1024), BF16),
            vmem((2, 256, 128), BF16),
            vmem((2, 2, 512, 128), F32),
            vmem((2, 2, 512, 128), F32),
            vmem((2, 2, 512, 128), F32),
            vmem((2, 2, 4, 64, 128), F32),
            vmem((2, 2, 64, 128), F32),
            vmem((2, 2, 2, 64, 128), F32),
            vmem((2, 2, 3, 64, 128), F32),
            vmem((2, 2, 3, 64, 128), F32),
            vmem((2, 2, 1024, 128), F32),
            vmem((2, 64, 128), F32),
            vmem((2, 64, 128), F32),
            vmem((2, 4, 64, 128), F32),
            vmem((2, 1024, 128), BF16),
            vmem((2, 2, 256, 128), F32),
            vmem((2, 2, 2, 32, 128), F32),
            vmem((2, 2, 2, 2, 32, 128), F32),
            vmem((2, 2, 2, 32, 128), F32),
            vmem((2, 128, 128), F32),
            vmem((2, 2048, 128), F32),
            dma((N_SEM,)),
            dma((N_SEM,)),
            dma((32,)),
        ],
        compiler_params=pltpu.CompilerParams(
            collective_id=0, has_side_effects=True, vmem_limit_bytes=40 * 2**20
        ),
        cost_estimate=pl.CostEstimate(flops=10**9, bytes_accessed=12 * 2**20, transcendentals=0),
    )(*(pltpu.with_memory_space_constraint(value, pltpu.HBM) for value in (observed, slip, green_left, green_right)), block_ranks, pltpu.with_memory_space_constraint(neighbours.T, pltpu.HBM))
    return pl.pallas_call(
        store,
        name="store",
        out_shape=shapes,
        in_specs=[whole, whole],
        out_specs=(hbm, hbm),
        scratch_shapes=[dma((2,))],
        compiler_params=pltpu.CompilerParams(vmem_limit_bytes=4 * 2**20),
    )(*(pltpu.with_memory_space_constraint(value, pltpu.VMEM) for value in joined))


def solution(mesh):
    return jax.shard_map(
        body,
        mesh=mesh,
        in_specs=(
            P("row", None),
            P("col", None),
            P("row", "col"),
            P("col", "row"),
            P("row", "col"),
            P("col", None),
        ),
        out_specs=(P("col", None), P("row", None)),
        check_vma=False,
    )
```
